32 devices in a mesh: wide: 8 (over z, x), narrow: 4 (over y, core).
Axes of the slice: x: 2, y: 2, z: 4, core: 2. Of those that a mesh axis runs over, the one named last changes fastest.
Arguments:
- inputs: bfloat16 [81920, 512], P(('wide', 'narrow')), may hold values from -6 to 6
- segments: int32 [81920], P(('wide', 'narrow')), may hold values from 0 to 8, as said below
- pad_mask: int32 [81920], P(('wide', 'narrow')), may hold values from 0 to 1, as said below
- cotangent: bfloat16 [81920, 512], P(('wide', 'narrow')), may hold values from -6 to 6
- w_query: bfloat16 [512, 512], P(None, ('wide', 'narrow')), may hold values from -0.25 to 0.25
- b_query: bfloat16 [512], P(('wide', 'narrow')), may hold values from -3 to 3
- w_key: bfloat16 [512, 512], P(None, ('wide', 'narrow')), may hold values from -0.25 to 0.25
- w_value: bfloat16 [512, 512], P(None, ('wide', 'narrow')), may hold values from -0.25 to 0.25
- b_value: bfloat16 [512], P(('wide', 'narrow')), may hold values from -3 to 3
- w_out: bfloat16 [512, 512], P(None, ('wide', 'narrow')), may hold values from -0.75 to 0.75
- b_out: bfloat16 [512], P(('wide', 'narrow')), may hold values from -2 to 2
- gain_one: bfloat16 [512], P(('wide', 'narrow')), may hold values from 0.25 to 1.75
- shift_one: bfloat16 [512], P(('wide', 'narrow')), may hold values from -3 to 3
- w_up: bfloat16 [512, 3200], P(('wide', 'narrow')), may hold values from -0.25 to 0.25
- b_up: bfloat16 [3200], P('narrow'), may hold values from -3 to 3
- w_down: bfloat16 [3200, 512], P(None, ('wide', 'narrow')), may hold values from -0.109375 to 0.109375
- b_down: bfloat16 [512], P(('wide', 'narrow')), may hold values from -2 to 2
- gain_two: bfloat16 [512], P(('wide', 'narrow')), may hold values from 0.25 to 1.75
- shift_two: bfloat16 [512], P(('wide', 'narrow')), may hold values from -3 to 3
- pos_table: bfloat16 [302, 512], P(None, ('wide', 'narrow')), may hold values from -3 to 3
Outputs:
- layer_out: bfloat16 [81920, 512], P(('wide', 'narrow'))
- input_grad: bfloat16 [81920, 512], P(('wide', 'narrow'))
- grad_w_query: float32 [512, 512], P(None, ('wide', 'narrow'))
- grad_b_query: float32 [512], P(('wide', 'narrow'))
- grad_w_key: float32 [512, 512], P(None, ('wide', 'narrow'))
- grad_w_value: float32 [512, 512], P(None, ('wide', 'narrow'))
- grad_b_value: float32 [512], P(('wide', 'narrow'))
- grad_w_out: float32 [512, 512], P(None, ('wide', 'narrow'))
- grad_b_out: float32 [512], P(('wide', 'narrow'))
- grad_gain_one: float32 [512], P(('wide', 'narrow'))
- grad_shift_one: float32 [512], P(('wide', 'narrow'))
- grad_w_up: float32 [512, 3200], P(('wide', 'narrow'))
- grad_b_up: float32 [3200], P('narrow')
- grad_w_down: float32 [3200, 512], P(None, ('wide', 'narrow'))
- grad_b_down: float32 [512], P(('wide', 'narrow'))
- grad_gain_two: float32 [512], P(('wide', 'narrow'))
- grad_shift_two: float32 [512], P(('wide', 'narrow'))
- grad_pos_table: float32 [302, 512], P(None, ('wide', 'narrow'))
The draws below stay inside these ranges and needn't reach their ends.
Inputs may be any that keep to these rules, and one draw needn't show every extreme that they name: `segments`: within each pack of 640 rows, items of 77 or 302 tokens follow one another from the pack's first row, numbered 0, 1, 2, ... in order; the rows after the last item, fewer than 302, carry the next number. `pad_mask`: 1 on the rows of a pack's items, 0 on the rows after them.
All inputs are finite; a program needn't handle non-finite values.
Results may differ from the reference program's by a relative error of at most 0.015.
The reference program's roundings to bfloat16 on the way count: a program that leaves them out, or rounds other values in their place, can miss the bound.
Values may be sent and summed in bfloat16 or wider, within the bound.
No kernel may reach another device: no remote copies, remote signals or barrier semaphores. Data moves between devices by JAX's collectives and lax.ppermute only.
A program may use at most 192 MiB of HBM per device.

```python
import math
import jax
import jax.numpy as jnp
from jax import lax

D = 512
H = 8
FF = 3200
HD = 64
PACK = 640
LONG = 302
SHORT = 77
TOK_DEV = 2560
TOKENS = 81920


def pack_layout(key):
    pack_count = TOKENS // PACK
    pack_kind = jax.random.randint(jax.random.fold_in(key, 11), (pack_count,), 0, 3)
    pack_kind = pack_kind.at[0].set(2).at[1].set(0)
    long_spot = jax.random.randint(jax.random.fold_in(key, 12), (pack_count,), 0, 5)
    slot_index = jnp.arange(8, dtype=jnp.int32)
    long_pair = jnp.where(slot_index < 2, LONG, 0)
    one_long = jnp.where(slot_index[None, :] < 5, jnp.where(slot_index[None, :] == long_spot[:, None], LONG, SHORT), 0)
    all_short = jnp.full((8,), SHORT, dtype=jnp.int32)
    kind_col = pack_kind[:, None]
    item_len = jnp.where(kind_col == 0, long_pair[None, :], jnp.where(kind_col == 1, one_long, all_short[None, :])).astype(jnp.int32)
    item_count = jnp.where(pack_kind == 0, 2, jnp.where(pack_kind == 1, 5, 8)).astype(jnp.int32)
    item_ends = jnp.cumsum(item_len, axis=1)
    row_index = jnp.arange(PACK, dtype=jnp.int32)
    live_slot = slot_index[None, None, :] < item_count[:, None, None]
    passed_end = (row_index[None, :, None] >= item_ends[:, None, :]) & live_slot
    seg_ids = jnp.sum(passed_end.astype(jnp.int32), axis=2)
    real_rows = jnp.max(jnp.where(slot_index[None, :] < item_count[:, None], item_ends, 0), axis=1)
    real_mask = (row_index[None, :] < real_rows[:, None]).astype(jnp.int32)
    return (seg_ids.reshape(-1).astype(jnp.int32), real_mask.reshape(-1).astype(jnp.int32))


def draw_segments(key, part):
    return pack_layout(key)[0]


def draw_pad_mask(key, part):
    return pack_layout(key)[1]


def spiked(values, stream_key, source, target, blocks, factor):
    def block_of(position):
        return (jnp.arange(values.shape[position]) // (values.shape[position] // blocks)).reshape((-1,) + (1,) * (values.ndim - 1 - position))

    first = jax.random.permutation(stream_key, blocks)[block_of(target)]
    other_side = (block_of(target) + blocks // 2) % blocks
    return jnp.where((block_of(source) == first) | (block_of(source) == other_side), factor * values, values)


def shard_levels(key, shape, pieces, least, top_value):
    factor_of, own = 1.0, jax.random.fold_in(key, 6)
    for axis_at, blocks in pieces:
        heights = jnp.exp(jax.random.uniform(jax.random.fold_in(own, axis_at), (blocks,), jnp.float32, least / len(pieces), top_value / len(pieces)))
        factor_of = factor_of * jnp.repeat(heights, shape[axis_at] // blocks).reshape([-1 if axis == axis_at else 1 for axis in range(len(shape))])
    return factor_of


def bell_draw(key, extent, width, most, shards=(), held_as=jnp.bfloat16):
    factor_of = shard_levels(key, extent, shards, -0.22, 0.18) if shards else 1.0
    values = jax.random.normal(key, extent, jnp.float32) * width * factor_of
    return jnp.minimum(jnp.maximum(values, -most), most).astype(held_as)


def noise_with(own_key, dims, width, most, split, heavy, kind=jnp.bfloat16):
    entries = width * jax.random.normal(own_key, dims, jnp.float32)
    if split:
        entries = entries * shard_levels(own_key, dims, split, -0.22, 0.18)
    return jnp.clip(spiked(entries, jax.random.fold_in(own_key, 3), *heavy), -most, most).astype(kind)


def setup_inputs(seed: int = 0) -> dict:
    key_list = jax.random.split(jax.random.key(seed), 21)
    return {
        "inputs": bell_draw(key_list[0], (TOKENS, D), 1.0, 6.0, ((0, 32),)),
        "segments": draw_segments(jax.random.fold_in(key_list[20], 71), 0),
        "pad_mask": draw_pad_mask(jax.random.fold_in(key_list[20], 71), 0),
        "cotangent": noise_with(key_list[3], (TOKENS, D), 1.0, 6.0, ((0, 32),), (0, 1, 32, 2.75)),
        "w_query": bell_draw(key_list[4], (D, D), D ** -0.5, 0.25, ((1, 32),)),
        "b_query": bell_draw(key_list[5], (D,), 0.5, 3.0, ((0, 32),)),
        "w_key": bell_draw(key_list[6], (D, D), D ** -0.5, 0.25, ((1, 32),)),
        "w_value": bell_draw(key_list[7], (D, D), D ** -0.5, 0.25, ((1, 32),)),
        "b_value": bell_draw(key_list[8], (D,), 0.5, 3.0, ((0, 32),)),
        "w_out": bell_draw(key_list[9], (D, D), (D // 8) ** -0.5, 0.75, ((1, 32),)),
        "b_out": bell_draw(key_list[10], (D,), 0.3, 2.0, ((0, 32),)),
        "gain_one": jnp.clip(1.0 + 0.15 * jax.random.normal(key_list[11], (D,), jnp.float32), 0.25, 1.75).astype(jnp.bfloat16),
        "shift_one": bell_draw(key_list[12], (D,), 0.5, 3.0, ((0, 32),)),
        "w_up": bell_draw(key_list[13], (D, FF), D ** -0.5, 0.25, ((0, 32),)),
        "b_up": bell_draw(key_list[14], (FF,), 0.5, 3.0, ((0, 4),)),
        "w_down": bell_draw(key_list[15], (FF, D), FF ** -0.5, 0.109375, ((1, 32),)),
        "b_down": bell_draw(key_list[16], (D,), 0.3, 2.0, ((0, 32),)),
        "gain_two": jnp.clip(1.0 + 0.15 * jax.random.normal(key_list[17], (D,), jnp.float32), 0.25, 1.75).astype(jnp.bfloat16),
        "shift_two": bell_draw(key_list[18], (D,), 0.5, 3.0, ((0, 32),)),
        "pos_table": bell_draw(key_list[19], (LONG, D), 0.5, 3.0, ((1, 32),)),
    }


@jax.custom_vjp
def low(v):
    return lax.optimization_barrier(v.astype(jnp.bfloat16)).astype(jnp.float32)

@jax.custom_vjp
def low_back(v):
    return v

def low_keep(v):
    return (low(v), None)

def low_pass(kept, grad):
    return (grad,)

def back_keep(v):
    return (v, None)

def back_low(kept, grad):
    return (low(grad),)
low.defvjp(low_keep, low_pass)
low_back.defvjp(back_keep, back_low)
exact_prec = lax.Precision.HIGHEST
eps_norm = 1e-05
neg_fill = -1000000000.0

def round_both(vector_in):
    return low(low_back(vector_in))

def matmul(left_op, right_op):
    return jnp.dot(left_op, right_op, precision=exact_prec)

def layout(seg_ids):
    row_index = jnp.arange(seg_ids.shape[0], dtype=jnp.int32)
    same_item = seg_ids[:, None] == seg_ids[None, :]
    first_row = lax.optimization_barrier(jnp.min(jnp.where(same_item, row_index[None, :], seg_ids.shape[0]), axis=1))
    return (same_item, (row_index - first_row).astype(jnp.int32))

def sinusoid(item_place, model_width):
    half_width = model_width // 2
    frequency = jnp.exp(jnp.arange(half_width, dtype=jnp.float32) * (-2.0 * math.log(10000.0) / model_width))
    angles = item_place.astype(jnp.float32)[:, None] * frequency[None, :]
    return jnp.concatenate([jnp.sin(angles), jnp.cos(angles)], axis=1)

def normalize(vector_in):
    centered = vector_in - lax.optimization_barrier(jnp.mean(vector_in, axis=-1, keepdims=True))
    variance = lax.optimization_barrier(jnp.mean(centered * centered, axis=-1, keepdims=True))
    return centered * lax.rsqrt(variance + eps_norm)

def attend(packed):
    query, keys, values, same_item = packed
    score_scale = 1.0 / math.sqrt(HD)
    q_heads = query.reshape(PACK, H, HD)
    k_heads = keys.reshape(PACK, H, HD)
    v_heads = values.reshape(PACK, H, HD)
    scores = jnp.einsum('qhd,khd->hqk', q_heads, k_heads, precision=exact_prec) * score_scale
    scores = low_back(scores)
    scores = jnp.where(same_item[None, :, :], scores, neg_fill)
    row_max = lax.optimization_barrier(jnp.max(scores, axis=-1, keepdims=True))
    exp_scores = jnp.exp(scores - row_max)
    attn_probs = low(exp_scores / lax.optimization_barrier(jnp.sum(exp_scores, axis=-1, keepdims=True)))
    mixed = jnp.einsum('hqk,khd->qhd', attn_probs, v_heads, precision=exact_prec)
    return mixed.reshape(PACK, D)

def forward(group_in, seg_group, keep_rows, w_query, b_query, w_key, w_value, b_value, w_out, b_out, gain_one, shift_one, w_up, b_up, w_down, b_down, gain_two, shift_two, pos_table):
    pack_count = group_in.shape[0] // PACK
    same_item, item_place = jax.vmap(layout)(seg_group.reshape(pack_count, PACK))
    item_place = item_place.reshape(-1)
    positions = sinusoid(item_place, D) + jnp.take(pos_table, item_place, axis=0)
    mixed_in = low(group_in + positions)
    query = round_both(matmul(mixed_in, w_query) + b_query)
    keys = round_both(matmul(mixed_in, w_key))
    values = round_both(matmul(group_in, w_value) + b_value)
    shaped = (query.reshape(pack_count, PACK, D), keys.reshape(pack_count, PACK, D), values.reshape(pack_count, PACK, D), same_item)
    attn = lax.map(jax.checkpoint(attend), shaped)
    attn = round_both(attn.reshape(-1, D))
    branch = low_back(matmul(attn, w_out) + b_out)
    hidden_first = gain_one * normalize(group_in + branch) + shift_one
    pre_act = low_back(matmul(low(hidden_first), w_up) + b_up)
    ff_out = low_back(matmul(low(jax.nn.gelu(pre_act)), w_down) + b_down)
    result = gain_two * normalize(hidden_first + ff_out) + shift_two
    return result * keep_rows[:, None]

def reference(inputs, segments, pad_mask, cotangent, w_query, b_query, w_key, w_value, b_value, w_out, b_out, gain_one, shift_one, w_up, b_up, w_down, b_down, gain_two, shift_two, pos_table):
    weights = tuple((weight_in.astype(jnp.float32) for weight_in in (w_query, b_query, w_key, w_value, b_value, w_out, b_out, gain_one, shift_one, w_up, b_up, w_down, b_down, gain_two, shift_two, pos_table)))
    groups = segments.shape[0] // TOK_DEV
    stacked = (inputs.astype(jnp.float32).reshape(groups, TOK_DEV, D), segments.reshape(groups, TOK_DEV), pad_mask.astype(jnp.float32).reshape(groups, TOK_DEV), cotangent.astype(jnp.float32).reshape(groups, TOK_DEV, D))

    def group_step(grad_total, group_item):
        group_in, seg_group, keep_rows, cot_group = group_item

        def layer_fn(layer_in, *params):
            return forward(layer_in, seg_group, keep_rows, *params)
        layer_val, pullback = jax.vjp(layer_fn, group_in, *weights)
        group_grads = pullback(cot_group)
        grad_total = tuple((earlier + addend for earlier, addend in zip(grad_total, group_grads[1:])))
        return (grad_total, (layer_val.astype(jnp.bfloat16), group_grads[0].astype(jnp.bfloat16)))
    zero_grads = tuple((jnp.zeros_like(weight_in) for weight_in in weights))
    grad_total, (layer_vals, input_vals) = lax.scan(group_step, zero_grads, stacked)
    layer_out = layer_vals.reshape(-1, D)
    input_grad = input_vals.reshape(-1, D)
    return (layer_out, input_grad, grad_total[0], grad_total[1], grad_total[2], grad_total[3], grad_total[4], grad_total[5], grad_total[6], grad_total[7], grad_total[8], grad_total[9], grad_total[10], grad_total[11], grad_total[12], grad_total[13], grad_total[14], grad_total[15])
```

```python
import math

import jax
import jax.numpy as jnp
from jax import lax
from jax.experimental import pallas as pl
from jax.experimental.pallas import tpu as pltpu
from jax.sharding import PartitionSpec as P

D = 512
H = 8
FF = 3200
HD = 64
PACK = 640
LONG = 302
PLACES = 384
SCALE = 0.125
EPS = 1e-05
NEG = -1e9
WT = 3 * D + PLACES
WA = WT + 128
BLOCK = 16
BLOCKS = D // BLOCK
WB = D + 2 * FF
TILE = 512
FF_CHUNKS = ((0, 768), (768, 768), (1536, 768), (2304, 896))
Q_CHUNKS = ((0, 256), (256, 256), (512, 128))
AXES = ("wide", "narrow")
VMEM = 60 * 1024 * 1024
BF = jnp.bfloat16
F32 = jnp.float32


def nn(a, b):
    return lax.dot_general(a, b, (((1,), (0,)), ((), ())), preferred_element_type=F32)


def nt(a, b):
    return lax.dot_general(a, b, (((1,), (1,)), ((), ())), preferred_element_type=F32)


def item_masks(seg_row):
    wide = jnp.broadcast_to(seg_row.astype(F32), (8, PACK))
    col = jnp.transpose(wide)[:, 0:1]
    return col == wide[0:1]


def head_lanes(block, half):
    lane = lax.broadcasted_iota(jnp.int32, block.shape, 1)
    keep = (lane < HD) if half == 0 else (lane >= HD)
    return jnp.where(keep, block, jnp.zeros_like(block))


def block_rows(me_ref, place):
    owner = me_ref[0] ^ offsets(BLOCKS)[place]
    return pl.ds(pl.multiple_of(owner * BLOCK, BLOCK), BLOCK)


def load_blocks(me_ref, halves, full_ref, sem):
    copies = []
    for place in range(BLOCKS):
        half, at = divmod(place, BLOCKS // 2)
        copies.append(pltpu.make_async_copy(halves[half].at[at * BLOCK : (at + 1) * BLOCK], full_ref.at[block_rows(me_ref, place)], sem))
    for copy in copies:
        copy.start()
    for copy in copies:
        copy.wait()


def store_blocks(me_ref, spans, halves, sem):
    copies = []
    for place in range(BLOCKS):
        half, at = divmod(place, BLOCKS // 2)
        for ref, col, width in spans:
            target = halves[half].at[at * BLOCK : (at + 1) * BLOCK, col : col + width]
            copies.append(pltpu.make_async_copy(ref.at[block_rows(me_ref, place)], target, sem))
    for copy in copies:
        copy.start()
    for copy in copies:
        copy.wait()


def attend_kernel(me_ref, seg_ref, x_ref, al_ref, ar_ref, st_ref, q_ref, k_ref, v_ref, mix_ref, attn_ref, pt_ref, vec_ref, ga_ref, hi_ref, lo_ref, bias_ref, vt_ref, at_ref, sem):
    @pl.when(pl.program_id(0) == 0)
    def _():
        load_blocks(me_ref, (al_ref, ar_ref), ga_ref, sem)
        vec_ref[...] = jnp.transpose(ga_ref[:, WT:].astype(F32))
        pos = st_ref[...] + ga_ref[:, 3 * D : 3 * D + PLACES].astype(F32)
        hi = pos.astype(BF)
        hi_ref[...] = hi
        lo_ref[...] = (pos - hi.astype(F32)).astype(BF)

    same = item_masks(seg_ref[0])
    bias_ref[...] = jnp.where(same, 0.0, NEG)
    lane = lax.broadcasted_iota(jnp.int32, (PACK, PACK), 1).astype(F32)
    first = jnp.min(jnp.where(same, lane, 1e6), axis=1, keepdims=True)
    place = lax.broadcasted_iota(jnp.int32, (PACK, 1), 0).astype(F32) - first
    slot = lax.broadcasted_iota(jnp.int32, (PACK, PLACES), 1).astype(F32)
    picks = jnp.where(place == slot, 1.0, 0.0).astype(BF)
    x = x_ref[...]
    positions = nt(picks, hi_ref[...]) + nt(picks, lo_ref[...])
    mixed = (x.astype(F32) + positions).astype(BF)
    mix_ref[...] = mixed
    q_ref[...] = ((nt(mixed, ga_ref[:, 0:D]) + vec_ref[0:1]).astype(BF).astype(F32) * SCALE).astype(BF)
    k_ref[...] = nt(mixed, ga_ref[:, D : 2 * D]).astype(BF)
    v = (nt(x, ga_ref[:, 2 * D : 3 * D]) + vec_ref[1:2]).astype(BF)
    v_ref[...] = v
    vt_ref[...] = jnp.transpose(v)

    def pair(j, carry):
        lanes = pl.ds(pl.multiple_of(j * 2 * HD, 2 * HD), 2 * HD)
        keys = k_ref[:, lanes]
        for half in range(2):
            rows = pl.ds(pl.multiple_of((2 * j + half) * HD, HD), HD)
            values_t = vt_ref[rows, :]
            for start, size in Q_CHUNKS:
                query = head_lanes(q_ref[start : start + size, lanes], half)
                scores = nt(keys, query) + bias_ref[:, start : start + size]
                top = jnp.max(scores, axis=0, keepdims=True)
                exps = jnp.exp(scores - top)
                total = jnp.sum(exps, axis=0, keepdims=True)
                probs = (exps * (1.0 / total)).astype(BF)
                pt_ref[0, 2 * j + half, :, start : start + size] = probs
                at_ref[rows, start : start + size] = nn(values_t, probs).astype(BF)
        return carry

    lax.fori_loop(0, H // 2, pair, 0)
    attn_ref[...] = jnp.transpose(at_ref[...])


def whole(shape):
    return pl.BlockSpec(shape, lambda i: tuple(0 for _ in shape), pipeline_mode=pl.Buffered(1))


def rows_of(count, width):
    return pl.BlockSpec((count, width), lambda i: (i, 0))


SCALAR = pl.BlockSpec(memory_space=pltpu.SMEM)
LOOSE = pl.BlockSpec(memory_space=pl.ANY)


def attend(where, seg, x, halves, st):
    packs = seg.shape[0]
    tokens = packs * PACK
    low = jax.ShapeDtypeStruct((tokens, D), BF)
    return pl.pallas_call(
        attend_kernel,
        grid=(packs,),
        in_specs=[SCALAR, pl.BlockSpec((1, 1, PACK), lambda i: (i, 0, 0)), rows_of(PACK, D), LOOSE, LOOSE, whole((D, PLACES))],
        out_specs=[rows_of(PACK, D)] * 5 + [pl.BlockSpec((1, H, PACK, PACK), lambda i: (i, 0, 0, 0)), whole((128, D))],
        out_shape=[low] * 5 + [jax.ShapeDtypeStruct((packs, H, PACK, PACK), BF), jax.ShapeDtypeStruct((128, D), F32)],
        scratch_shapes=[
            pltpu.VMEM((D, WA), BF),
            pltpu.VMEM((D, PLACES), BF),
            pltpu.VMEM((D, PLACES), BF),
            pltpu.VMEM((PACK, PACK), F32),
            pltpu.VMEM((D, PACK), BF),
            pltpu.VMEM((D, PACK), BF),
            pltpu.SemaphoreType.DMA,
        ],
        compiler_params=pltpu.CompilerParams(vmem_limit_bytes=VMEM),
        cost_estimate=pl.CostEstimate(flops=40 * 10**9, bytes_accessed=50 * 10**6, transcendentals=0),
        name="attend",
    )(where, seg, x, *halves, st)


def centre(v):
    c = v - jnp.mean(v, axis=-1, keepdims=True)
    r = lax.rsqrt(jnp.mean(c * c, axis=-1, keepdims=True) + EPS)
    return c * r, r


def norm_back(g, n, r):
    return r * (g - jnp.mean(g, axis=-1, keepdims=True) - n * jnp.mean(g * n, axis=-1, keepdims=True))


def col_sum(v):
    return jnp.sum(v, axis=0, keepdims=True)


GELU_A = math.sqrt(2.0 / math.pi)
GELU_B = 0.044715


def feed_kernel(me_ref, x_ref, attn_ref, cot_ref, pad_ref, bl_ref, br_ref, vec_ref, bup_ref, out_ref, dfirst_ref, dattn_ref, keep_ref, send_ref, gv_ref, gbu_ref, gb_ref, act_ref, slope_ref, up_acc, down_acc, wo_acc, wo_low, sem):
    step = pl.program_id(0)

    @pl.when(step == 0)
    def _():
        load_blocks(me_ref, (bl_ref, br_ref), gb_ref, sem)
        up_acc[...] = jnp.zeros_like(up_acc)
        down_acc[...] = jnp.zeros_like(down_acc)
        wo_acc[...] = jnp.zeros_like(wo_acc)
        gv_ref[...] = jnp.zeros_like(gv_ref)
        gbu_ref[...] = jnp.zeros_like(gbu_ref)

    keep = jnp.transpose(jnp.broadcast_to(pad_ref[0].astype(F32), (8, TILE)))[:, 0:1]
    attn = attn_ref[...]
    gain_one, gain_two = vec_ref[3:4], vec_ref[6:7]
    first_sum = x_ref[...].astype(F32) + (nt(attn, gb_ref[:, 0:D]) + vec_ref[2:3])
    norm_one, r_one = centre(first_sum)
    hidden = gain_one * norm_one + vec_ref[4:5]
    hidden_low = hidden.astype(BF)
    hidden_t = jnp.transpose(hidden_low)
    ff = jnp.zeros((TILE, D), F32)
    for start, size in FF_CHUNKS:
        cols = slice(start, start + size)
        u = nn(hidden_low, gb_ref[:, D + start : D + start + size]) + bup_ref[0:1, cols]
        u2 = u * u
        t = jnp.tanh(u * (GELU_A + GELU_A * GELU_B * u2))
        h = 0.5 + 0.5 * t
        act = (u * h).astype(BF)
        act_ref[:, cols] = act
        slope_ref[:, cols] = (h + (u * h) * (1.0 - t) * (GELU_A + 3.0 * GELU_A * GELU_B * u2)).astype(BF)
        ff = ff + nt(act, gb_ref[:, D + FF + start : D + FF + start + size])
    norm_two, r_two = centre(hidden + (ff + vec_ref[5:6]))
    out_ref[...] = ((gain_two * norm_two + vec_ref[7:8]) * keep).astype(BF)
    top = cot_ref[...].astype(F32) * keep
    gv_ref[6:7] += col_sum(top * norm_two)
    gv_ref[7:8] += col_sum(top)
    d_second = norm_back(top * gain_two, norm_two, r_two)
    d_ff = d_second.astype(BF)
    gv_ref[5:6] += col_sum(d_ff.astype(F32))
    d_ff_t = jnp.transpose(d_ff)
    d_hidden = d_second
    for start, size in FF_CHUNKS:
        cols = slice(start, start + size)
        d_act = nn(d_ff, gb_ref[:, D + FF + start : D + FF + start + size])
        d_pre = (slope_ref[:, cols].astype(F32) * d_act).astype(BF)
        gbu_ref[0:1, cols] += col_sum(d_pre.astype(F32))
        down_acc[:, cols] += nn(d_ff_t, act_ref[:, cols])
        up_acc[:, cols] += nn(hidden_t, d_pre)
        d_hidden = d_hidden + nt(d_pre, gb_ref[:, D + start : D + start + size])
    gv_ref[3:4] += col_sum(d_hidden * norm_one)
    gv_ref[4:5] += col_sum(d_hidden)
    d_first = norm_back(d_hidden * gain_one, norm_one, r_one)
    dfirst_ref[...] = d_first
    d_branch = d_first.astype(BF)
    gv_ref[2:3] += col_sum(d_branch.astype(F32))
    wo_acc[...] += nn(jnp.transpose(d_branch), attn)
    dattn_ref[...] = nn(d_branch, gb_ref[:, 0:D]).astype(BF)

    @pl.when(step == pl.num_programs(0) - 1)
    def _():
        wo_low[...] = wo_acc[...].astype(BF)
        act_ref[...] = up_acc[...].astype(BF)
        slope_ref[...] = down_acc[...].astype(BF)
        spans = ((wo_low, 0, D), (act_ref, D, FF), (slope_ref, D + FF, FF))
        store_blocks(me_ref, spans, (keep_ref, send_ref), sem)


def feed(where, x, attn, cot, pad, halves, vec, bup):
    tokens = x.shape[0]
    return pl.pallas_call(
        feed_kernel,
        grid=(tokens // TILE,),
        in_specs=[
            SCALAR,
            rows_of(TILE, D),
            rows_of(TILE, D),
            rows_of(TILE, D),
            pl.BlockSpec((1, 1, TILE), lambda i: (i, 0, 0)),
            LOOSE,
            LOOSE,
            whole((128, D)),
            whole((1, FF)),
        ],
        out_specs=[rows_of(TILE, D), rows_of(TILE, D), rows_of(TILE, D), LOOSE, LOOSE, whole((8, D)), whole((1, FF))],
        out_shape=[
            jax.ShapeDtypeStruct((tokens, D), BF),
            jax.ShapeDtypeStruct((tokens, D), F32),
            jax.ShapeDtypeStruct((tokens, D), BF),
            jax.ShapeDtypeStruct((D // 2, WB), BF),
            jax.ShapeDtypeStruct((D // 2, WB), BF),
            jax.ShapeDtypeStruct((8, D), F32),
            jax.ShapeDtypeStruct((1, FF), F32),
        ],
        scratch_shapes=[
            pltpu.VMEM((D, WB), BF),
            pltpu.VMEM((TILE, FF), BF),
            pltpu.VMEM((TILE, FF), BF),
            pltpu.VMEM((D, FF), F32),
            pltpu.VMEM((D, FF), F32),
            pltpu.VMEM((D, D), F32),
            pltpu.VMEM((D, D), BF),
            pltpu.SemaphoreType.DMA,
        ],
        compiler_params=pltpu.CompilerParams(vmem_limit_bytes=VMEM),
        cost_estimate=pl.CostEstimate(flops=80 * 10**9, bytes_accessed=40 * 10**6, transcendentals=0),
        name="feed",
    )(where, x, attn, cot, pad.reshape(tokens // TILE, 1, TILE), *halves, vec, bup)


def back_kernel(me_ref, seg_ref, x_ref, q_ref, k_ref, v_ref, mix_ref, dattn_ref, dfirst_ref, pt_ref, al_ref, ar_ref, gv_ref, extra_ref, ig_ref, keep_ref, send_ref, ga_ref, gw_ref, ds_ref, kt_ref, dqt_ref, dk_ref, dv_ref, q_acc, k_acc, v_acc, t_acc, b_acc, sem):
    step = pl.program_id(0)

    @pl.when(step == 0)
    def _():
        load_blocks(me_ref, (al_ref, ar_ref), ga_ref, sem)
        for acc in (q_acc, k_acc, v_acc, t_acc):
            acc[...] = jnp.zeros_like(acc)
        b_acc[...] = gv_ref[...]

    kt_ref[...] = jnp.transpose(k_ref[...])

    def pair(j, carry):
        lanes = pl.ds(pl.multiple_of(j * 2 * HD, 2 * HD), 2 * HD)
        d_keys = jnp.zeros((PACK, 2 * HD), F32)
        d_values = jnp.zeros((PACK, 2 * HD), F32)
        for half in range(2):
            head = 2 * j + half
            rows = pl.ds(pl.multiple_of(head * HD, HD), HD)
            values = head_lanes(v_ref[:, lanes], half)
            for start, size in Q_CHUNKS:
                cols = slice(start, start + size)
                probs = pt_ref[0, head, :, cols].astype(F32)
                d_probs = nt(values, dattn_ref[cols, lanes])
                delta = jnp.sum(probs * d_probs, axis=0, keepdims=True)
                d_scores = (probs * (d_probs - delta)).astype(BF)
                ds_ref[half, :, cols] = d_scores
                dqt_ref[rows, cols] = (nn(kt_ref[rows, :], d_scores) * SCALE).astype(BF)
            d_values = d_values + nn(pt_ref[0, head], head_lanes(dattn_ref[:, lanes], half))
            d_keys = d_keys + nn(ds_ref[half], head_lanes(q_ref[:, lanes], half))
        dk_ref[:, lanes] = d_keys.astype(BF)
        dv_ref[:, lanes] = d_values.astype(BF)
        return carry

    lax.fori_loop(0, H // 2, pair, 0)
    dq_t = dqt_ref[...]
    dq = jnp.transpose(dq_t)
    dk = dk_ref[...]
    dv = dv_ref[...]
    mixed = mix_ref[...]
    q_acc[...] += nn(dq_t, mixed)
    k_acc[...] += nn(jnp.transpose(dk), mixed)
    v_acc[...] += nn(jnp.transpose(dv), x_ref[...])
    b_acc[0:1] += col_sum(dq.astype(F32))
    b_acc[1:2] += col_sum(dv.astype(F32))
    d_mixed = nn(dq, ga_ref[:, 0:D]) + nn(dk, ga_ref[:, D : 2 * D])
    same = item_masks(seg_ref[0])
    sub = lax.broadcasted_iota(jnp.int32, (PACK, PACK), 0).astype(F32)
    first = jnp.min(jnp.where(same, sub, 1e6), axis=0, keepdims=True)
    place = lax.broadcasted_iota(jnp.int32, (1, PACK), 1).astype(F32) - first
    slot = lax.broadcasted_iota(jnp.int32, (PLACES, PACK), 0).astype(F32)
    picks_t = jnp.where(place == slot, 1.0, 0.0).astype(BF)
    t_acc[...] += nn(picks_t, d_mixed.astype(BF))
    ig_ref[...] = (dfirst_ref[...] + d_mixed + nn(dv, ga_ref[:, 2 * D : 3 * D])).astype(BF)

    @pl.when(step == pl.num_programs(0) - 1)
    def _():
        gw_ref[:, 0:D] = q_acc[...].astype(BF)
        gw_ref[:, D : 2 * D] = k_acc[...].astype(BF)
        gw_ref[:, 2 * D : 3 * D] = v_acc[...].astype(BF)
        gw_ref[:, 3 * D : WT] = jnp.transpose(t_acc[...]).astype(BF)
        extra = extra_ref[...]
        vec = jnp.concatenate([b_acc[...], jnp.zeros((extra.shape[1] - 8, D), F32)], axis=0)
        gw_ref[:, WT:] = (jnp.transpose(vec) + extra).astype(BF)
        store_blocks(me_ref, ((gw_ref, 0, gw_ref.shape[1]),), (keep_ref, send_ref), sem)


def back(where, seg, x, q, k, v, mixed, d_attn, d_first, pt, halves, gv, extra):
    packs = seg.shape[0]
    width = WT + extra.shape[1]
    tokens = packs * PACK
    return pl.pallas_call(
        back_kernel,
        grid=(packs,),
        in_specs=[SCALAR, pl.BlockSpec((1, 1, PACK), lambda i: (i, 0, 0))]
        + [rows_of(PACK, D)] * 7
        + [pl.BlockSpec((1, H, PACK, PACK), lambda i: (i, 0, 0, 0)), LOOSE, LOOSE, whole((8, D)), whole(extra.shape)],
        out_specs=[rows_of(PACK, D), LOOSE, LOOSE],
        out_shape=[jax.ShapeDtypeStruct((tokens, D), BF)] + [jax.ShapeDtypeStruct((D // 2, width), BF)] * 2,
        scratch_shapes=[
            pltpu.VMEM((D, WA), BF),
            pltpu.VMEM((D, width), BF),
            pltpu.VMEM((2, PACK, PACK), BF),
            pltpu.VMEM((D, PACK), BF),
            pltpu.VMEM((D, PACK), BF),
            pltpu.VMEM((PACK, D), BF),
            pltpu.VMEM((PACK, D), BF),
            pltpu.VMEM((D, D), F32),
            pltpu.VMEM((D, D), F32),
            pltpu.VMEM((D, D), F32),
            pltpu.VMEM((PLACES, D), F32),
            pltpu.VMEM((8, D), F32),
            pltpu.SemaphoreType.DMA,
        ],
        compiler_params=pltpu.CompilerParams(vmem_limit_bytes=VMEM),
        cost_estimate=pl.CostEstimate(flops=60 * 10**9, bytes_accessed=50 * 10**6, transcendentals=0),
        name="back",
    )(where, seg, x, q, k, v, mixed, d_attn, d_first, pt, *halves, gv, extra)


def sines():
    half = D // 2
    frequency = jnp.exp(jnp.arange(half, dtype=F32) * (-2.0 * math.log(10000.0) / D))
    angles = frequency[:, None] * jnp.arange(PLACES, dtype=F32)[None, :]
    return jnp.concatenate([jnp.sin(angles), jnp.cos(angles)], axis=0)


def bit_groups(count):
    bits = count.bit_length() - 1
    return [(0,)] + [tuple(range(at, min(at + 2, bits))) for at in range(1, bits, 2)]


def offsets(count):
    found = [0]
    for group in bit_groups(count):
        found = [old | mask for old in found for mask in masks(group)]
    return found


def masks(group):
    return [index << group[0] for index in range(1 << len(group))]


def swap(block, mask, count):
    return lax.ppermute(block, AXES, [(i, i ^ mask) for i in range(count)])


def gather_phase(own, group, count):
    return [own] + [swap(own, mask, count) for mask in masks(group)[1:]]


def scatter_phase(pieces, group, count):
    total = pieces[0].astype(F32)
    for piece, mask in zip(pieces[1:], masks(group)[1:]):
        total = total + swap(piece, mask, count).astype(F32)
    return total


def split_rows(block, count):
    rows = block.shape[0] // count
    return [block[at * rows : (at + 1) * rows] for at in range(count)]


def scatter_rest(block, groups, count):
    for group in groups:
        block = scatter_phase(split_rows(block.astype(BF), 1 << len(group)), group, count)
    return block


def local(
    inputs,
    segments,
    pad_mask,
    cotangent,
    w_query,
    b_query,
    w_key,
    w_value,
    b_value,
    w_out,
    b_out,
    gain_one,
    shift_one,
    w_up,
    b_up,
    w_down,
    b_down,
    gain_two,
    shift_two,
    pos_table,
):
    tokens = inputs.shape[0]
    narrow = lax.axis_size("narrow")
    wide = lax.axis_size("wide")
    count = wide * narrow
    me = lax.axis_index(AXES)
    groups = bit_groups(count)
    own_rows = D // count
    bits = count.bit_length() - 1
    places = [bits - 1 - bit for group in groups for bit in reversed(group)] + [bits, bits + 1]
    in_kernel = own_rows == BLOCK
    where = (me if in_kernel else jnp.zeros((), jnp.int32)).reshape(1).astype(jnp.int32)

    def flips(full):
        for axis in range(bits):
            mine = (me >> (bits - 1 - axis)) & 1
            full = jnp.where(mine == 1, jnp.flip(full, axis), full)
        return full

    def absolute(halves):
        if in_kernel:
            return halves
        full = jnp.concatenate(halves, axis=0).reshape([2] * bits + [own_rows, -1])
        full = flips(full.transpose([places.index(axis) for axis in range(bits + 2)])).reshape(D, -1)
        return full[: D // 2], full[D // 2 :]

    def relative(halves):
        if in_kernel:
            return halves
        full = flips(jnp.concatenate(halves, axis=0).reshape([2] * bits + [own_rows, -1]))
        full = full.transpose(places).reshape(D, -1)
        return full[: D // 2], full[D // 2 :]

    seg = segments.reshape(tokens // PACK, 1, PACK)
    bias_width = b_up.shape[0]
    bias_piece = -(-bias_width // wide)
    piece_cols = -(-bias_piece // own_rows)
    bias_own = jnp.pad(b_up, (0, bias_piece * wide - bias_width))
    bias_own = lax.dynamic_slice_in_dim(bias_own, lax.axis_index("wide") * bias_piece, bias_piece)
    bias_own = jnp.pad(bias_own, (0, piece_cols * own_rows - bias_piece)).reshape(piece_cols, own_rows)
    rows = jnp.stack([b_query, b_value, b_out, gain_one, shift_one, b_down, gain_two, shift_two], axis=0)
    rows = jnp.concatenate([rows, bias_own, jnp.zeros((120 - piece_cols, own_rows), BF)], axis=0)
    table = jnp.pad(pos_table, ((0, PLACES - LONG), (0, 0)))
    own_a = jnp.concatenate([w_query, w_key, w_value, table, rows], axis=0).T
    own_b = jnp.concatenate([w_out.T, w_up, w_down.T], axis=1)

    for group in reversed(groups[1:]):
        own_a = jnp.concatenate(gather_phase(own_a, group, count), axis=0)
    a_halves = absolute(tuple(gather_phase(own_a, groups[0], count)))
    for group in reversed(groups[1:]):
        own_b = jnp.concatenate(gather_phase(own_b, group, count), axis=0)
    b_halves = absolute(tuple(gather_phase(own_b, groups[0], count)))

    q, k, v, mixed, attn, pt, vec = attend(where, seg, inputs, a_halves, sines())
    bup = vec[8 : 8 + piece_cols].reshape(piece_cols, wide, narrow, own_rows)
    bup = bup.transpose(2, 1, 0, 3).reshape(narrow, wide, piece_cols * own_rows)[:, :, :bias_piece]
    bup = bup.reshape(narrow, wide * bias_piece)[:, :bias_width].reshape(1, FF)
    layer_out, d_first, d_attn, keep_b, send_b, gv, gbu = feed(where, inputs, attn, cotangent, pad_mask, b_halves, vec, bup)
    grad_cols = -(-bias_width // own_rows)
    extra = jnp.pad(gbu.reshape(narrow, bias_width), ((0, 0), (0, grad_cols * own_rows - bias_width)))
    extra = jnp.broadcast_to(extra.reshape(1, narrow, own_rows, grad_cols), (wide, narrow, own_rows, grad_cols))
    extra_width = -(-(8 + grad_cols) // 128) * 128
    extra = jnp.pad(extra.reshape(D, grad_cols), ((0, 0), (8, extra_width - 8 - grad_cols)))
    own_grad_b = scatter_phase(relative((keep_b, send_b)), groups[0], count)
    own_grad_b = scatter_rest(own_grad_b, groups[1:], count)
    input_grad, keep_a, send_a = back(where, seg, inputs, q, k, v, mixed, d_attn, d_first, pt, a_halves, gv, extra)
    own_grad_a = scatter_phase(relative((keep_a, send_a)), groups[0], count)
    own_grad_a = scatter_rest(own_grad_a, groups[1:], count)
    grad_b_up = own_grad_a[:, WT + 8 : WT + 8 + grad_cols].reshape(grad_cols * own_rows)[:bias_width]
    own_vec = own_grad_a[:, WT : WT + 8]
    return (
        layer_out,
        input_grad,
        own_grad_a[:, 0:D].T,
        own_vec[:, 0],
        own_grad_a[:, D : 2 * D].T,
        own_grad_a[:, 2 * D : 3 * D].T,
        own_vec[:, 1],
        own_grad_b[:, 0:D].T,
        own_vec[:, 2],
        own_vec[:, 3],
        own_vec[:, 4],
        own_grad_b[:, D : D + FF],
        grad_b_up,
        own_grad_b[:, D + FF :].T,
        own_vec[:, 5],
        own_vec[:, 6],
        own_vec[:, 7],
        own_grad_a[:, 3 * D : 3 * D + LONG].T,
    )


def solution(mesh):
    both = P(("wide", "narrow"))
    rows = P(("wide", "narrow"), None)
    cols = P(None, ("wide", "narrow"))
    in_specs = (rows, both, both, rows, cols, both, cols, cols, both, cols, both, both, both, rows, P("narrow"), cols, both, both, both, cols)
    out_specs = (rows, rows, cols, both, cols, cols, both, cols, both, both, both, rows, P("narrow"), cols, both, both, both, cols)
    return jax.shard_map(local, mesh=mesh, in_specs=in_specs, out_specs=out_specs, check_vma=False)
```

```python
import functools
import math

import jax
import jax.numpy as jnp
import numpy as np
from jax import lax
from jax.experimental import pallas as pl
from jax.experimental.pallas import tpu as pltpu
from jax.sharding import PartitionSpec as P

D = 512
H = 8
FF = 3200
HD = 64
PACK = 640
LONG = 302
PLACES = 384
SCALE = 0.125
EPS = 1e-05
NEG = -1e9
WT = 3 * D + PLACES
WA = WT + 128
BLOCK = 16
BLOCKS = D // BLOCK
WB = D + 2 * FF
TILE = 512
FF_CHUNKS = ((0, 768), (768, 768), (1536, 768), (2304, 896))
ITEMS = 9
SHORT_WINDOW = (96, 128)
LONG_WINDOW = (320, 384)
SHORT_MOST = SHORT_WINDOW[0] - 15
PROB_ROWS = 1024
GROUP = 4
GROUPS = H // GROUP
GD = GROUP * HD
PROB_COLS = GROUP * LONG_WINDOW[1]
AXES = ("wide", "narrow")
VMEM = 60 * 1024 * 1024
BF = jnp.bfloat16
F32 = jnp.float32


def nn(a, b):
    return lax.dot_general(a, b, (((1,), (0,)), ((), ())), preferred_element_type=F32)


def nt(a, b):
    return lax.dot_general(a, b, (((1,), (1,)), ((), ())), preferred_element_type=F32)


def item_masks(seg_row):
    wide = jnp.broadcast_to(seg_row.astype(F32), (8, PACK))
    col = jnp.transpose(wide)[:, 0:1]
    return col == wide[0:1]


def place_picks(same):
    lane = lax.broadcasted_iota(jnp.int32, (PACK, PACK), 1).astype(F32)
    first = jnp.min(jnp.where(same, lane, 1e6), axis=1, keepdims=True)
    place = lax.broadcasted_iota(jnp.int32, (PACK, 1), 0).astype(F32) - first
    slot = lax.broadcasted_iota(jnp.int32, (PACK, PLACES), 1).astype(F32)
    return jnp.where(place == slot, 1.0, 0.0).astype(BF)


def each_item(starts_ref, pack, body):
    def visit(n, place):
        first = starts_ref[pack * (ITEMS + 1) + n]
        end = starts_ref[pack * (ITEMS + 1) + n + 1]
        length = end - first

        def window(sizes):
            spans = []
            for size in sizes:
                base = pl.multiple_of(jnp.minimum(lax.div(first, 16) * 16, PACK - size), 16)
                spans.append((size, pl.ds(base, size), first - base, end - base))
            body(*spans, pl.ds(pl.multiple_of(place, 16), sizes[0]))

        short = length <= SHORT_MOST

        @pl.when((length > 0) & short)
        def _():
            window(SHORT_WINDOW)

        @pl.when(length > SHORT_MOST)
        def _():
            window(LONG_WINDOW)

        return place + jnp.where(length > 0, jnp.where(short, SHORT_WINDOW[0], LONG_WINDOW[0]), 0)

    lax.fori_loop(0, ITEMS, visit, jnp.int32(0))


def by_head(block):
    lane = lax.broadcasted_iota(jnp.int32, block.shape, 1)
    zero = jnp.zeros_like(block)
    return jnp.concatenate([jnp.where((lane >= h * HD) & (lane < (h + 1) * HD), block, zero) for h in range(GROUP)], axis=0)


def heads_turned(left_t, right, size):
    parts = [nn(left_t[h * HD : (h + 1) * HD], right[:, h * size : (h + 1) * size]) for h in range(GROUP)]
    return jnp.concatenate(parts, axis=0)


GROUP_LANES = [slice(g * GD, (g + 1) * GD) for g in range(GROUPS)]


def block_rows(me_ref, place):
    owner = me_ref[0] ^ offsets(BLOCKS)[place]
    return pl.ds(pl.multiple_of(owner * BLOCK, BLOCK), BLOCK)


def load_blocks(me_ref, halves, full_ref, sem):
    copies = []
    for place in range(BLOCKS):
        half, at = divmod(place, BLOCKS // 2)
        copies.append(pltpu.make_async_copy(halves[half].at[at * BLOCK : (at + 1) * BLOCK], full_ref.at[block_rows(me_ref, place)], sem))
    for copy in copies:
        copy.start()
    for copy in copies:
        copy.wait()


def store_blocks(me_ref, spans, halves, sem):
    copies = []
    for place in range(BLOCKS):
        half, at = divmod(place, BLOCKS // 2)
        for ref, col, width in spans:
            target = halves[half].at[at * BLOCK : (at + 1) * BLOCK, col : col + width]
            copies.append(pltpu.make_async_copy(ref.at[block_rows(me_ref, place)], target, sem))
    for copy in copies:
        copy.start()
    for copy in copies:
        copy.wait()


def attend_kernel(me_ref, starts_ref, seg_ref, x_ref, al_ref, ar_ref, st_ref, q_ref, k_ref, v_ref, mix_ref, attn_ref, pt_ref, vec_ref, pieces_ref, ga_ref, hi_ref, lo_ref, sem):
    @pl.when(pl.program_id(0) == 0)
    def _():
        load_blocks(me_ref, (al_ref, ar_ref), ga_ref, sem)
        pieces_ref[...] = ga_ref[:, WT:].astype(F32)
        vec_ref[...] = jnp.transpose(pieces_ref[...])
        pos = st_ref[...] + ga_ref[:, 3 * D : 3 * D + PLACES].astype(F32)
        hi = pos.astype(BF)
        hi_ref[...] = hi
        lo_ref[...] = (pos - hi.astype(F32)).astype(BF)

    same = item_masks(seg_ref[...])
    picks = place_picks(same)
    x = x_ref[...]
    positions = nt(picks, hi_ref[...]) + nt(picks, lo_ref[...])
    mixed = (x.astype(F32) + positions).astype(BF)
    mix_ref[...] = mixed
    q_ref[...] = ((nt(mixed, ga_ref[:, 0:D]) + vec_ref[0:1]).astype(BF).astype(F32) * SCALE).astype(BF)
    k_ref[...] = nt(mixed, ga_ref[:, D : 2 * D]).astype(BF)
    v = (nt(x, ga_ref[:, 2 * D : 3 * D]) + vec_ref[1:2]).astype(BF)
    v_ref[...] = v
    attn_ref[...] = jnp.zeros_like(attn_ref)

    def item(key_span, query_span, store):
        keys, key_rows, low, high = key_span
        down = lax.broadcasted_iota(jnp.int32, (keys, 1), 0)
        shut = jnp.where((down >= low) & (down < high), 0.0, NEG)
        queries, query_rows, low, high = query_span
        across = lax.broadcasted_iota(jnp.int32, (1, queries), 1)
        live = jnp.where((across >= low) & (across < high), 1.0, 0.0)
        live = jnp.concatenate([live] * GROUP, axis=1)
        scores = [nt(k_ref[key_rows, lanes], by_head(q_ref[query_rows, lanes])) + shut for lanes in GROUP_LANES]
        probs = []
        for g in range(GROUPS):
            exps = jnp.exp(scores[g] - jnp.max(scores[g], axis=0, keepdims=True))
            scale = live / jnp.sum(exps, axis=0, keepdims=True)
            probs.append((exps * scale).astype(BF))
            pt_ref[0, g, store, 0 : GROUP * queries] = probs[g]
        for g, lanes in enumerate(GROUP_LANES):
            outs = heads_turned(jnp.transpose(v_ref[key_rows, lanes]), probs[g], queries)
            attn_ref[query_rows, lanes] += jnp.transpose(outs.astype(BF))

    each_item(starts_ref, pl.program_id(0), item)


def whole(shape):
    return pl.BlockSpec(shape, lambda i: tuple(0 for _ in shape), pipeline_mode=pl.Buffered(1))


def rows_of(count, width):
    return pl.BlockSpec((count, width), lambda i: (i, 0))


SCALAR = pl.BlockSpec(memory_space=pltpu.SMEM)
LOOSE = pl.BlockSpec(memory_space=pl.ANY)


def attend(where, starts, seg, x, halves, st):
    tokens = seg.shape[1]
    packs = tokens // PACK
    low = jax.ShapeDtypeStruct((tokens, D), BF)
    return pl.pallas_call(
        attend_kernel,
        grid=(packs,),
        in_specs=[SCALAR, SCALAR, pl.BlockSpec((1, PACK), lambda i: (0, i)), rows_of(PACK, D), LOOSE, LOOSE, whole((D, PLACES))],
        out_specs=[rows_of(PACK, D)] * 5 + [pl.BlockSpec((1, GROUPS, PROB_ROWS, PROB_COLS), lambda i: (i, 0, 0, 0)), whole((128, D)), whole((D, 128))],
        out_shape=[low] * 5
        + [jax.ShapeDtypeStruct((packs, GROUPS, PROB_ROWS, PROB_COLS), BF), jax.ShapeDtypeStruct((128, D), F32), jax.ShapeDtypeStruct((D, 128), F32)],
        scratch_shapes=[
            pltpu.VMEM((D, WA), BF),
            pltpu.VMEM((D, PLACES), BF),
            pltpu.VMEM((D, PLACES), BF),
            pltpu.SemaphoreType.DMA,
        ],
        compiler_params=pltpu.CompilerParams(vmem_limit_bytes=VMEM),
        cost_estimate=pl.CostEstimate(flops=40 * 10**9, bytes_accessed=50 * 10**6, transcendentals=0),
        name="attend",
    )(where, starts, seg, x, *halves, st)


def centre(v):
    c = v - jnp.mean(v, axis=-1, keepdims=True)
    r = lax.rsqrt(jnp.mean(c * c, axis=-1, keepdims=True) + EPS)
    return c * r, r


def norm_back(g, n, r):
    return r * (g - jnp.mean(g, axis=-1, keepdims=True) - n * jnp.mean(g * n, axis=-1, keepdims=True))


def col_sum(v):
    return jnp.sum(v, axis=0, keepdims=True)


GELU_A = math.sqrt(2.0 / math.pi)
GELU_B = 0.044715


def feed_kernel(me_ref, x_ref, attn_ref, cot_ref, pad_ref, gb_ref, vec_ref, bup_ref, out_ref, dfirst_ref, dattn_ref, keep_ref, send_ref, gv_ref, gbu_ref, act_ref, slope_ref, up_acc, down_acc, wo_acc, wo_low, sem):
    step = pl.program_id(0)

    @pl.when(step == 0)
    def _():
        up_acc[...] = jnp.zeros_like(up_acc)
        down_acc[...] = jnp.zeros_like(down_acc)
        wo_acc[...] = jnp.zeros_like(wo_acc)
        gv_ref[...] = jnp.zeros_like(gv_ref)
        gbu_ref[...] = jnp.zeros_like(gbu_ref)

    keep = jnp.transpose(jnp.broadcast_to(pad_ref[...].astype(F32), (8, TILE)))[:, 0:1]
    attn = attn_ref[...]
    gain_one, gain_two = vec_ref[3:4], vec_ref[6:7]
    first_sum = x_ref[...].astype(F32) + (nt(attn, gb_ref[:, 0:D]) + vec_ref[2:3])
    norm_one, r_one = centre(first_sum)
    hidden = gain_one * norm_one + vec_ref[4:5]
    hidden_low = hidden.astype(BF)
    hidden_t = jnp.transpose(hidden_low)
    ff = jnp.zeros((TILE, D), F32)
    for start, size in FF_CHUNKS:
        cols = slice(start, start + size)
        u = nn(hidden_low, gb_ref[:, D + start : D + start + size]) + bup_ref[0:1, cols]
        u2 = u * u
        t = jnp.tanh(u * (GELU_A + GELU_A * GELU_B * u2))
        h = 0.5 + 0.5 * t
        act = (u * h).astype(BF)
        act_ref[:, cols] = act
        slope_ref[:, cols] = (h + (u * h) * (1.0 - t) * (GELU_A + 3.0 * GELU_A * GELU_B * u2)).astype(BF)
        ff = ff + nt(act, gb_ref[:, D + FF + start : D + FF + start + size])
    norm_two, r_two = centre(hidden + (ff + vec_ref[5:6]))
    out_ref[...] = ((gain_two * norm_two + vec_ref[7:8]) * keep).astype(BF)
    top = cot_ref[...].astype(F32) * keep
    gv_ref[6:7] += col_sum(top * norm_two)
    gv_ref[7:8] += col_sum(top)
    d_second = norm_back(top * gain_two, norm_two, r_two)
    d_ff = d_second.astype(BF)
    gv_ref[5:6] += col_sum(d_ff.astype(F32))
    d_ff_t = jnp.transpose(d_ff)
    d_hidden = d_second
    for start, size in FF_CHUNKS:
        cols = slice(start, start + size)
        d_act = nn(d_ff, gb_ref[:, D + FF + start : D + FF + start + size])
        d_pre = (slope_ref[:, cols].astype(F32) * d_act).astype(BF)
        gbu_ref[0:1, cols] += col_sum(d_pre.astype(F32))
        down_acc[:, cols] += nn(d_ff_t, act_ref[:, cols])
        up_acc[:, cols] += nn(hidden_t, d_pre)
        d_hidden = d_hidden + nt(d_pre, gb_ref[:, D + start : D + start + size])
    gv_ref[3:4] += col_sum(d_hidden * norm_one)
    gv_ref[4:5] += col_sum(d_hidden)
    d_first = norm_back(d_hidden * gain_one, norm_one, r_one)
    dfirst_ref[...] = d_first
    d_branch = d_first.astype(BF)
    gv_ref[2:3] += col_sum(d_branch.astype(F32))
    wo_acc[...] += nn(jnp.transpose(d_branch), attn)
    dattn_ref[...] = nn(d_branch, gb_ref[:, 0:D]).astype(BF)

    @pl.when(step == pl.num_programs(0) - 1)
    def _():
        wo_low[...] = wo_acc[...].astype(BF)
        act_ref[...] = up_acc[...].astype(BF)
        slope_ref[...] = down_acc[...].astype(BF)
        spans = ((wo_low, 0, D), (act_ref, D, FF), (slope_ref, D + FF, FF))
        store_blocks(me_ref, spans, (keep_ref, send_ref), sem)


def feed(where, x, attn, cot, pad, gb, vec, bup):
    tokens = x.shape[0]
    return pl.pallas_call(
        feed_kernel,
        grid=(tokens // TILE,),
        in_specs=[
            SCALAR,
            rows_of(TILE, D),
            rows_of(TILE, D),
            rows_of(TILE, D),
            pl.BlockSpec((1, TILE), lambda i: (0, i)),
            whole((D, WB)),
            whole((128, D)),
            whole((1, FF)),
        ],
        out_specs=[rows_of(TILE, D), rows_of(TILE, D), rows_of(TILE, D), LOOSE, LOOSE, whole((8, D)), whole((1, FF))],
        out_shape=[
            jax.ShapeDtypeStruct((tokens, D), BF),
            jax.ShapeDtypeStruct((tokens, D), F32),
            jax.ShapeDtypeStruct((tokens, D), BF),
            jax.ShapeDtypeStruct((D // 2, WB), BF),
            jax.ShapeDtypeStruct((D // 2, WB), BF),
            jax.ShapeDtypeStruct((8, D), F32),
            jax.ShapeDtypeStruct((1, FF), F32),
        ],
        scratch_shapes=[
            pltpu.VMEM((TILE, FF), BF),
            pltpu.VMEM((TILE, FF), BF),
            pltpu.VMEM((D, FF), F32),
            pltpu.VMEM((D, FF), F32),
            pltpu.VMEM((D, D), F32),
            pltpu.VMEM((D, D), BF),
            pltpu.SemaphoreType.DMA,
        ],
        compiler_params=pltpu.CompilerParams(vmem_limit_bytes=VMEM),
        cost_estimate=pl.CostEstimate(flops=80 * 10**9, bytes_accessed=40 * 10**6, transcendentals=0),
        name="feed",
    )(where, x, attn, cot, pad.reshape(1, tokens), gb, vec, bup)


def tn(a, b):
    return lax.dot_general(a, b, (((0,), (0,)), ((), ())), preferred_element_type=F32)


def core_kernel(first_pack, starts_ref, q_ref, k_ref, v_ref, dattn_ref, pt_ref, *refs):
    dq_ref, dk_ref, dv_ref, dqt_ref, dkt_ref, dvt_ref = refs[-6:]
    for ref in (dq_ref, dk_ref, dv_ref):
        ref[...] = jnp.zeros_like(ref)

    def item(key_span, query_span, store):
        key_rows = key_span[1]
        queries, query_rows = query_span[:2]
        d_outs = [by_head(dattn_ref[query_rows, lanes]) for lanes in GROUP_LANES]
        d_probs = [nt(v_ref[key_rows, lanes], d_outs[g]) for g, lanes in enumerate(GROUP_LANES)]
        probs = [pt_ref[0, g, store, 0 : GROUP * queries] for g in range(GROUPS)]
        d_scores = []
        for g in range(GROUPS):
            wide = probs[g].astype(F32)
            delta = jnp.sum(wide * d_probs[g], axis=0, keepdims=True)
            d_scores.append((wide * (d_probs[g] - delta)).astype(BF))
        for g, lanes in enumerate(GROUP_LANES):
            dv_ref[key_rows, lanes] += nn(probs[g], d_outs[g]).astype(BF)
            dk_ref[key_rows, lanes] += nn(d_scores[g], by_head(q_ref[query_rows, lanes])).astype(BF)
            d_queries = heads_turned(jnp.transpose(k_ref[key_rows, lanes]), d_scores[g], queries) * SCALE
            dq_ref[query_rows, lanes] += jnp.transpose(d_queries.astype(BF))

    each_item(starts_ref, pl.program_id(0) + first_pack, item)
    dqt_ref[0] = jnp.transpose(dq_ref[...])
    dkt_ref[0] = jnp.transpose(dk_ref[...])
    dvt_ref[0] = jnp.transpose(dv_ref[...])


def core_back(first, steps, starts, q, k, v, d_attn, pt, earlier=(), after=()):
    tokens = q.shape[0]
    packs = tokens // PACK
    flat = pl.BlockSpec((PACK, D), lambda i: (i + first, 0))
    turned = pl.BlockSpec((1, D, PACK), lambda i: (i + first, 0, 0))
    shapes = [jax.ShapeDtypeStruct((tokens, D), BF)] * 3 + [jax.ShapeDtypeStruct((packs, D, PACK), BF)] * 3
    return pl.pallas_call(
        functools.partial(core_kernel, first),
        grid=(steps,),
        in_specs=[SCALAR] + [flat] * 4 + [pl.BlockSpec((1, GROUPS, PROB_ROWS, PROB_COLS), lambda i: (i + first, 0, 0, 0))] + [LOOSE] * (len(earlier) + len(after)),
        out_specs=[flat] * 3 + [turned] * 3,
        out_shape=shapes,
        input_output_aliases={6 + n: n for n in range(len(earlier))},
        compiler_params=pltpu.CompilerParams(vmem_limit_bytes=VMEM),
        cost_estimate=pl.CostEstimate(flops=18 * 10**9 * steps, bytes_accessed=12 * 10**6 * steps, transcendentals=0),
        name="core_back",
    )(starts, q, k, v, d_attn, pt, *earlier, *after)


def grads_kernel(me_ref, seg_ref, x_ref, mix_ref, dqt_ref, dkt_ref, dvt_ref, al_ref, ar_ref, gv_ref, extra_ref, *refs):
    keep_ref, send_ref, ga_ref, gw_ref, q_acc, k_acc, v_acc, tq_acc, tk_acc, b_acc, sem = refs[-11:]
    step = pl.program_id(0)

    @pl.when(step == 0)
    def _():
        load_blocks(me_ref, (al_ref, ar_ref), ga_ref, sem)
        for acc in (q_acc, k_acc, v_acc, tq_acc, tk_acc, b_acc):
            acc[...] = jnp.zeros_like(acc)

    dq_t, dk_t, dv_t = dqt_ref[0], dkt_ref[0], dvt_ref[0]
    mixed = mix_ref[...]
    picks = place_picks(item_masks(seg_ref[...]))
    q_acc[...] += nn(dq_t, mixed)
    k_acc[...] += nn(dk_t, mixed)
    v_acc[...] += nn(dv_t, x_ref[...])
    tq_acc[...] += nn(dq_t, picks)
    tk_acc[...] += nn(dk_t, picks)
    lane = lax.broadcasted_iota(jnp.int32, (1, 128), 1)
    b_acc[...] += jnp.where(lane == 0, jnp.sum(dq_t.astype(F32), axis=1, keepdims=True), 0.0)
    b_acc[...] += jnp.where(lane == 1, jnp.sum(dv_t.astype(F32), axis=1, keepdims=True), 0.0)

    @pl.when(step == pl.num_programs(0) - 1)
    def _():
        gw_ref[:, 0:D] = q_acc[...].astype(BF)
        gw_ref[:, D : 2 * D] = k_acc[...].astype(BF)
        gw_ref[:, 2 * D : 3 * D] = v_acc[...].astype(BF)
        table = tn(ga_ref[:, 0:D], tq_acc[...].astype(BF)) + tn(ga_ref[:, D : 2 * D], tk_acc[...].astype(BF))
        gw_ref[:, 3 * D : WT] = table.astype(BF)
        vec = jnp.concatenate([gv_ref[...], jnp.zeros((120, D), F32)], axis=0)
        gw_ref[:, WT : WT + 128] = (jnp.transpose(vec) + b_acc[...] + extra_ref[:, 0:128]).astype(BF)
        for at in range(128, extra_ref.shape[1], 128):
            gw_ref[:, WT + at : WT + at + 128] = extra_ref[:, at : at + 128].astype(BF)
        store_blocks(me_ref, ((gw_ref, 0, gw_ref.shape[1]),), (keep_ref, send_ref), sem)


def grads(where, seg, x, mixed, turned, halves, gv, extra, after):
    packs = seg.shape[1] // PACK
    width = WT + extra.shape[1]
    return pl.pallas_call(
        grads_kernel,
        grid=(packs,),
        in_specs=[SCALAR, pl.BlockSpec((1, PACK), lambda i: (0, i))]
        + [rows_of(PACK, D)] * 2
        + [pl.BlockSpec((1, D, PACK), lambda i: (i, 0, 0))] * 3
        + [LOOSE, LOOSE, whole((8, D)), whole(extra.shape)]
        + [LOOSE] * len(after),
        out_specs=[LOOSE, LOOSE],
        out_shape=[jax.ShapeDtypeStruct((D // 2, width), BF)] * 2,
        scratch_shapes=[
            pltpu.VMEM((D, WA), BF),
            pltpu.VMEM((D, width), BF),
            pltpu.VMEM((D, D), F32),
            pltpu.VMEM((D, D), F32),
            pltpu.VMEM((D, D), F32),
            pltpu.VMEM((D, PLACES), F32),
            pltpu.VMEM((D, PLACES), F32),
            pltpu.VMEM((D, 128), F32),
            pltpu.SemaphoreType.DMA,
        ],
        compiler_params=pltpu.CompilerParams(vmem_limit_bytes=VMEM),
        cost_estimate=pl.CostEstimate(flops=10 * 10**9, bytes_accessed=20 * 10**6, transcendentals=0),
        name="grads",
    )(where, seg, x, mixed, *turned, *halves, gv, extra, *after)


def inputs_kernel(me_ref, dq_ref, dk_ref, dv_ref, dfirst_ref, al_ref, ar_ref, after_ref, out_ref, ga_ref, sem):
    @pl.when(pl.program_id(0) == 0)
    def _():
        load_blocks(me_ref, (al_ref, ar_ref), ga_ref, sem)

    d_mixed = nn(dq_ref[...], ga_ref[:, 0:D]) + nn(dk_ref[...], ga_ref[:, D : 2 * D])
    out_ref[...] = (dfirst_ref[...] + d_mixed + nn(dv_ref[...], ga_ref[:, 2 * D : 3 * D])).astype(BF)


def input_grads(where, flat, d_first, halves, after):
    tokens = d_first.shape[0]
    return pl.pallas_call(
        inputs_kernel,
        grid=(tokens // PACK,),
        in_specs=[SCALAR] + [rows_of(PACK, D)] * 4 + [LOOSE, LOOSE, LOOSE],
        out_specs=rows_of(PACK, D),
        out_shape=jax.ShapeDtypeStruct((tokens, D), BF),
        scratch_shapes=[pltpu.VMEM((D, WA), BF), pltpu.SemaphoreType.DMA],
        compiler_params=pltpu.CompilerParams(vmem_limit_bytes=VMEM),
        cost_estimate=pl.CostEstimate(flops=8 * 10**9, bytes_accessed=20 * 10**6, transcendentals=0),
        name="input_grads",
    )(where, *flat, d_first, *halves, after)


def sines():
    half = D // 2
    frequency = np.exp(np.arange(half, dtype=np.float32) * np.float32(-2.0 * math.log(10000.0) / D))
    angles = frequency[:, None] * np.arange(PLACES, dtype=np.float32)[None, :]
    return jnp.asarray(np.concatenate([np.sin(angles), np.cos(angles)], axis=0).astype(np.float32))


def pack_kernel(piece, wide_ref, wq_ref, wk_ref, wv_ref, table_ref, wo_ref, up_ref, down_ref, bup_ref, *refs):
    vectors, (a_ref, b_ref, turn_ref, bias_ref) = refs[:8], refs[8:]
    rows = a_ref.shape[0]
    a_ref[:, 0:D] = wq_ref[...]
    a_ref[:, D : 2 * D] = wk_ref[...]
    a_ref[:, 2 * D : 3 * D] = wv_ref[...]
    a_ref[:, 3 * D : WT] = jnp.zeros((rows, PLACES), BF)
    a_ref[:, 3 * D : 3 * D + LONG] = table_ref[...]
    b_ref[:, 0:D] = wo_ref[...]
    b_ref[:, D : D + FF] = up_ref[...]
    b_ref[:, D + FF :] = down_ref[...]
    turn_ref[...] = jnp.zeros_like(turn_ref)
    for n, vector in enumerate(vectors):
        turn_ref[n : n + 1, 0:rows] = vector[...].astype(F32)
    bias_ref[...] = jnp.zeros_like(bias_ref)
    bias_ref[0:1, 0 : bup_ref.shape[1]] = bup_ref[...].astype(F32)
    span = bias_ref.shape[1]
    shift = lax.rem(span + 8 - wide_ref[0] * piece, span)
    moved = pltpu.roll(bias_ref[...], shift, 1)[0:1, 0:128]
    lane = lax.broadcasted_iota(jnp.int32, (rows, 128), 1)
    row = lax.broadcasted_iota(jnp.int32, (rows, 128), 0)
    mine = (row == 0) & (lane >= 8) & (lane < 8 + piece)
    columns = jnp.transpose(turn_ref[...])[0:rows]
    a_ref[:, WT:] = jnp.where(mine, moved, columns).astype(BF)


def pack(wide_index, piece, matrices, b_up, vectors):
    rows = matrices[0].shape[0]
    span = -(-(b_up.shape[0] + 8) // 128) * 128
    return pl.pallas_call(
        functools.partial(pack_kernel, piece),
        in_specs=[SCALAR] + [pl.BlockSpec(memory_space=pltpu.VMEM)] * 16,
        out_specs=[pl.BlockSpec(memory_space=pltpu.VMEM)] * 2,
        out_shape=[jax.ShapeDtypeStruct((rows, WA), BF), jax.ShapeDtypeStruct((rows, WB), BF)],
        scratch_shapes=[pltpu.VMEM((128, 128), F32), pltpu.VMEM((8, span), F32)],
        name="pack",
    )(wide_index.reshape(1), *matrices, b_up.reshape(1, -1), *[vector.reshape(1, rows) for vector in vectors])


def bit_groups(count):
    bits = count.bit_length() - 1
    return [(0,)] + [tuple(range(at, min(at + 2, bits))) for at in range(1, bits, 2)]


def offsets(count):
    found = [0]
    for group in bit_groups(count):
        found = [old | mask for old in found for mask in masks(group)]
    return found


def masks(group):
    return [index << group[0] for index in range(1 << len(group))]


def swap(block, mask, count):
    return lax.ppermute(block, AXES, [(i, i ^ mask) for i in range(count)])


def gather_phase(own, group, count):
    return [own] + [swap(own, mask, count) for mask in masks(group)[1:]]


def scatter_phase(pieces, group, count):
    total = pieces[0].astype(F32)
    for piece, mask in zip(pieces[1:], masks(group)[1:]):
        total = total + swap(piece, mask, count).astype(F32)
    return total


def split_rows(block, count):
    rows = block.shape[0] // count
    return [block[at * rows : (at + 1) * rows] for at in range(count)]


def scatter_rest(block, groups, count):
    for group in groups:
        block = scatter_phase(split_rows(block.astype(BF), 1 << len(group)), group, count)
    return block


def local(
    inputs,
    segments,
    pad_mask,
    cotangent,
    w_query,
    b_query,
    w_key,
    w_value,
    b_value,
    w_out,
    b_out,
    gain_one,
    shift_one,
    w_up,
    b_up,
    w_down,
    b_down,
    gain_two,
    shift_two,
    pos_table,
):
    tokens = inputs.shape[0]
    narrow = lax.axis_size("narrow")
    wide = lax.axis_size("wide")
    count = wide * narrow
    me = lax.axis_index(AXES)
    groups = bit_groups(count)
    own_rows = D // count
    bits = count.bit_length() - 1
    places = [bits - 1 - bit for group in groups for bit in reversed(group)] + [bits, bits + 1]
    in_kernel = own_rows == BLOCK
    where = (me if in_kernel else jnp.zeros((), jnp.int32)).reshape(1).astype(jnp.int32)

    def flips(full):
        for axis in range(bits):
            mine = (me >> (bits - 1 - axis)) & 1
            full = jnp.where(mine == 1, jnp.flip(full, axis), full)
        return full

    def absolute(halves):
        if in_kernel:
            return halves
        full = jnp.concatenate(halves, axis=0).reshape([2] * bits + [own_rows, -1])
        full = flips(full.transpose([places.index(axis) for axis in range(bits + 2)])).reshape(D, -1)
        return full[: D // 2], full[D // 2 :]

    def relative(halves):
        if in_kernel:
            return halves
        full = flips(jnp.concatenate(halves, axis=0).reshape([2] * bits + [own_rows, -1]))
        full = full.transpose(places).reshape(D, -1)
        return full[: D // 2], full[D // 2 :]

    seg = segments.reshape(1, tokens)
    packs = tokens // PACK
    below = segments.reshape(packs, 1, PACK) < jnp.arange(ITEMS + 1, dtype=jnp.int32)[None, :, None]
    starts = jnp.sum(below.astype(jnp.int32), axis=2).reshape(packs * (ITEMS + 1))
    bias_width = b_up.shape[0]
    bias_piece = -(-bias_width // wide)
    own_a, own_b = pack(
        lax.axis_index("wide").astype(jnp.int32),
        bias_piece,
        (w_query.T, w_key.T, w_value.T, pos_table.T, w_out.T, w_up, w_down.T),
        b_up,
        (b_query, b_value, b_out, gain_one, shift_one, b_down, gain_two, shift_two),
    )
    gb = lax.all_gather(own_b, AXES, axis=0, tiled=True)
    for group in reversed(groups[1:]):
        own_a = jnp.concatenate(gather_phase(own_a, group, count), axis=0)
    a_halves = absolute(tuple(gather_phase(own_a, groups[0], count)))
    q, k, v, mixed, attn, pt, vec, pieces = attend(where, starts, seg, inputs, a_halves, sines())
    bup = pieces.reshape(wide, narrow, own_rows, 128)[:, :, 0, 8 : 8 + bias_piece].transpose(1, 0, 2)
    bup = bup.reshape(narrow, wide * bias_piece)[:, :bias_width].reshape(1, FF)
    layer_out, d_first, d_attn, keep_b, send_b, gv, gbu = feed(where, inputs, attn, cotangent, pad_mask, gb, vec, bup)
    grad_cols = -(-bias_width // own_rows)
    extra = jnp.pad(gbu.reshape(narrow, bias_width), ((0, 0), (0, grad_cols * own_rows - bias_width)))
    extra = jnp.broadcast_to(extra.reshape(1, narrow, own_rows, grad_cols), (wide, narrow, own_rows, grad_cols))
    extra_width = -(-(8 + grad_cols) // 128) * 128
    extra = jnp.pad(extra.reshape(D, grad_cols), ((0, 0), (8, extra_width - 8 - grad_cols)))
    early = packs // 2
    back = core_back(0, early, starts, q, k, v, d_attn, pt)
    sum_b = scatter_phase(relative((keep_b, send_b)), groups[0], count).astype(BF)
    parts_b = split_rows(sum_b, 1 << len(groups[1]))
    back = core_back(early, packs - early, starts, q, k, v, d_attn, pt, back, parts_b)
    sum_b = scatter_phase(parts_b, groups[1], count).astype(BF)
    parts_b = split_rows(sum_b, 1 << len(groups[2]))
    keep_a, send_a = grads(where, seg, inputs, mixed, back[3:], a_halves, gv, extra, parts_b)
    own_grad_b = scatter_rest(scatter_phase(parts_b, groups[2], count), groups[3:], count)
    input_grad = input_grads(where, back[:3], d_first, a_halves, keep_a)
    own_grad_a = scatter_phase(relative((keep_a, send_a)), groups[0], count)
    own_grad_a = scatter_rest(own_grad_a, groups[1:], count)
    grad_b_up = own_grad_a[:, WT + 8 : WT + 8 + grad_cols].reshape(grad_cols * own_rows)[:bias_width]
    own_vec = own_grad_a[:, WT : WT + 8]
    return (
        layer_out,
        input_grad,
        own_grad_a[:, 0:D].T,
        own_vec[:, 0],
        own_grad_a[:, D : 2 * D].T,
        own_grad_a[:, 2 * D : 3 * D].T,
        own_vec[:, 1],
        own_grad_b[:, 0:D].T,
        own_vec[:, 2],
        own_vec[:, 3],
        own_vec[:, 4],
        own_grad_b[:, D : D + FF],
        grad_b_up,
        own_grad_b[:, D + FF :].T,
        own_vec[:, 5],
        own_vec[:, 6],
        own_vec[:, 7],
        own_grad_a[:, 3 * D : 3 * D + LONG].T,
    )


def solution(mesh):
    both = P(("wide", "narrow"))
    rows = P(("wide", "narrow"), None)
    cols = P(None, ("wide", "narrow"))
    in_specs = (rows, both, both, rows, cols, both, cols, cols, both, cols, both, both, both, rows, P("narrow"), cols, both, both, both, cols)
    out_specs = (rows, rows, cols, both, cols, cols, both, cols, both, both, both, rows, P("narrow"), cols, both, both, both, cols)
    return jax.shard_map(local, mesh=mesh, in_specs=in_specs, out_specs=out_specs, check_vma=False)
```

```python
import functools
import math

import jax
import jax.numpy as jnp
import numpy as np
from jax import lax
from jax.experimental import pallas as pl
from jax.experimental.pallas import tpu as pltpu
from jax.sharding import PartitionSpec as P

D = 512
H = 8
FF = 3200
HD = 64
PACK = 640
LONG = 302
PLACES = 384
SCALE = 0.125
EPS = 1e-05
NEG = -1e9
WT = 3 * D + PLACES
WA = WT + 128
BLOCK = 16
BLOCKS = D // BLOCK
PIECES = 4
PIECE = D // (2 * PIECES)
WB = D + 2 * FF
TILE = 512
PARTS = 1
FF_CHUNKS = ((0, 1536), (1536, 1664))
ITEMS = 9
SHORT_WINDOW = (96, 128)
LONG_WINDOW = (320, 384)
SHORT_MOST = SHORT_WINDOW[0] - 15
PROB_ROWS = 1024
GROUP = 4
GROUPS = H // GROUP
GD = GROUP * HD
PROB_COLS = GROUP * LONG_WINDOW[1]
AXES = ("wide", "narrow")
VMEM = 60 * 1024 * 1024
BF = jnp.bfloat16
F32 = jnp.float32


def nn(a, b):
    return lax.dot_general(a, b, (((1,), (0,)), ((), ())), preferred_element_type=F32)


def nt(a, b):
    return lax.dot_general(a, b, (((1,), (1,)), ((), ())), preferred_element_type=F32)


def item_masks(seg_row):
    wide = jnp.broadcast_to(seg_row.astype(F32), (8, PACK))
    col = jnp.transpose(wide)[:, 0:1]
    return col == wide[0:1]


def place_picks(same):
    lane = lax.broadcasted_iota(jnp.int32, (PACK, PACK), 1).astype(F32)
    first = jnp.min(jnp.where(same, lane, 1e6), axis=1, keepdims=True)
    place = lax.broadcasted_iota(jnp.int32, (PACK, 1), 0).astype(F32) - first
    slot = lax.broadcasted_iota(jnp.int32, (PACK, PLACES), 1).astype(F32)
    return jnp.where((place == slot) | (slot == PLACES - 1), 1.0, 0.0).astype(BF)


def each_item(starts_ref, pack, body):
    def visit(n, place):
        first = starts_ref[pack * (ITEMS + 1) + n]
        end = starts_ref[pack * (ITEMS + 1) + n + 1]
        length = end - first

        def window(sizes):
            spans = []
            for size in sizes:
                base = pl.multiple_of(jnp.minimum(lax.div(first, 16) * 16, PACK - size), 16)
                spans.append((size, pl.ds(base, size), first - base, end - base))
            body(*spans, pl.ds(pl.multiple_of(place, 16), sizes[0]))

        short = length <= SHORT_MOST

        @pl.when((length > 0) & short)
        def _():
            window(SHORT_WINDOW)

        @pl.when(length > SHORT_MOST)
        def _():
            window(LONG_WINDOW)

        return place + jnp.where(length > 0, jnp.where(short, SHORT_WINDOW[0], LONG_WINDOW[0]), 0)

    lax.fori_loop(0, ITEMS, visit, jnp.int32(0))


def by_head(block):
    lane = lax.broadcasted_iota(jnp.int32, block.shape, 1)
    zero = jnp.zeros_like(block)
    return jnp.concatenate([jnp.where((lane >= h * HD) & (lane < (h + 1) * HD), block, zero) for h in range(GROUP)], axis=0)


def heads_turned(left_t, right, size):
    parts = [nn(left_t[h * HD : (h + 1) * HD], right[:, h * size : (h + 1) * size]) for h in range(GROUP)]
    return jnp.concatenate(parts, axis=0)


GROUP_LANES = [slice(g * GD, (g + 1) * GD) for g in range(GROUPS)]


def block_rows(me_ref, place):
    owner = me_ref[0] ^ offsets(BLOCKS)[place]
    return pl.ds(pl.multiple_of(owner * BLOCK, BLOCK), BLOCK)


def block_loads(me_ref, halves, full_ref, sem):
    copies = []
    for place in range(BLOCKS):
        half, at = divmod(place, BLOCKS // 2)
        copies.append(pltpu.make_async_copy(halves[half].at[at * BLOCK : (at + 1) * BLOCK], full_ref.at[block_rows(me_ref, place)], sem))
    return copies


def load_blocks(me_ref, halves, full_ref, sem):
    copies = block_loads(me_ref, halves, full_ref, sem)
    for copy in copies:
        copy.start()
    for copy in copies:
        copy.wait()


def block_copies(me_ref, ref, col, width, pieces, sem):
    copies = []
    for place in range(BLOCKS):
        piece, at = divmod(place * BLOCK, PIECE)
        target = pieces[piece].at[at : at + BLOCK, col : col + width]
        copies.append(pltpu.make_async_copy(ref.at[block_rows(me_ref, place)], target, sem))
    return copies


def store_blocks(me_ref, ref, pieces, sem):
    copies = block_copies(me_ref, ref, 0, ref.shape[1], pieces, sem)
    for copy in copies:
        copy.start()
    for copy in copies:
        copy.wait()


def attend_kernel(me_ref, starts_ref, seg_ref, x_ref, al_ref, ar_ref, st_ref, q_ref, k_ref, v_ref, mix_ref, attn_ref, picks_ref, pt_ref, vec_ref, pieces_ref, ga_ref, hi_ref, lo_ref, sem):
    @pl.when(pl.program_id(0) == 0)
    def _():
        load_blocks(me_ref, (al_ref, ar_ref), ga_ref, sem)
        pieces_ref[...] = ga_ref[:, WT:].astype(F32)
        vec_ref[...] = jnp.transpose(pieces_ref[...])
        pos = st_ref[...] + ga_ref[:, 3 * D : 3 * D + PLACES].astype(F32)
        pos = jnp.where(lax.broadcasted_iota(jnp.int32, pos.shape, 1) < LONG, pos, 0.0)
        hi = pos.astype(BF)
        hi_ref[...] = hi
        lo_ref[...] = (pos - hi.astype(F32)).astype(BF)

    picks = place_picks(item_masks(seg_ref[...]))
    picks_ref[...] = picks
    x = x_ref[...]
    positions = nt(picks, hi_ref[...]) + nt(picks, lo_ref[...])
    mixed = (x.astype(F32) + positions).astype(BF)
    mix_ref[...] = mixed
    q_ref[...] = ((nt(mixed, ga_ref[:, 0:D]) + vec_ref[0:1]).astype(BF).astype(F32) * SCALE).astype(BF)
    k_ref[...] = nt(mixed, ga_ref[:, D : 2 * D]).astype(BF)
    v = (nt(x, ga_ref[:, 2 * D : 3 * D]) + vec_ref[1:2]).astype(BF)
    v_ref[...] = v
    attn_ref[...] = jnp.zeros_like(attn_ref)

    def item(key_span, query_span, store):
        keys, key_rows, low, high = key_span
        down = lax.broadcasted_iota(jnp.int32, (keys, 1), 0)
        shut = jnp.where((down >= low) & (down < high), 0.0, NEG)
        queries, query_rows, low, high = query_span
        across = lax.broadcasted_iota(jnp.int32, (1, queries), 1)
        live = jnp.where((across >= low) & (across < high), 1.0, 0.0)
        live = jnp.concatenate([live] * GROUP, axis=1)
        scores = [nt(k_ref[key_rows, lanes], by_head(q_ref[query_rows, lanes])) + shut for lanes in GROUP_LANES]
        probs = []
        for g in range(GROUPS):
            exps = jnp.exp(scores[g] - jnp.max(scores[g], axis=0, keepdims=True))
            scale = live / jnp.sum(exps, axis=0, keepdims=True)
            probs.append((exps * scale).astype(BF))
            pt_ref[0, g, store, 0 : GROUP * queries] = probs[g]
        for g, lanes in enumerate(GROUP_LANES):
            outs = heads_turned(jnp.transpose(v_ref[key_rows, lanes]), probs[g], queries)
            attn_ref[query_rows, lanes] += jnp.transpose(outs.astype(BF))

    each_item(starts_ref, pl.program_id(0), item)


def whole(shape):
    return pl.BlockSpec(shape, lambda i: tuple(0 for _ in shape), pipeline_mode=pl.Buffered(1))


def rows_of(count, width):
    return pl.BlockSpec((count, width), lambda i: (i, 0))


SCALAR = pl.BlockSpec(memory_space=pltpu.SMEM)
LOOSE = pl.BlockSpec(memory_space=pl.ANY)


def attend(where, starts, seg, x, halves, st):
    tokens = seg.shape[1]
    packs = tokens // PACK
    low = jax.ShapeDtypeStruct((tokens, D), BF)
    return pl.pallas_call(
        attend_kernel,
        grid=(packs,),
        in_specs=[SCALAR, SCALAR, pl.BlockSpec((1, PACK), lambda i: (0, i)), rows_of(PACK, D), LOOSE, LOOSE, whole((D, PLACES))],
        out_specs=[rows_of(PACK, D)] * 5 + [rows_of(PACK, PLACES), pl.BlockSpec((1, GROUPS, PROB_ROWS, PROB_COLS), lambda i: (i, 0, 0, 0)), whole((128, D)), whole((D, 128))],
        out_shape=[low] * 5
        + [
            jax.ShapeDtypeStruct((tokens, PLACES), BF),
            jax.ShapeDtypeStruct((packs, GROUPS, PROB_ROWS, PROB_COLS), BF), jax.ShapeDtypeStruct((128, D), F32), jax.ShapeDtypeStruct((D, 128), F32)],
        scratch_shapes=[
            pltpu.VMEM((D, WA), BF),
            pltpu.VMEM((D, PLACES), BF),
            pltpu.VMEM((D, PLACES), BF),
            pltpu.SemaphoreType.DMA,
        ],
        compiler_params=pltpu.CompilerParams(vmem_limit_bytes=VMEM),
        cost_estimate=pl.CostEstimate(flops=40 * 10**9, bytes_accessed=50 * 10**6, transcendentals=0),
        name="attend",
    )(where, starts, seg, x, *halves, st)


def centre(v):
    c = v - jnp.mean(v, axis=-1, keepdims=True)
    r = lax.rsqrt(jnp.mean(c * c, axis=-1, keepdims=True) + EPS)
    return c * r, r


def norm_back(g, n, r):
    return r * (g - jnp.mean(g, axis=-1, keepdims=True) - n * jnp.mean(g * n, axis=-1, keepdims=True))


def col_sum(v):
    return jnp.sum(v, axis=0, keepdims=True)


GELU_A = math.sqrt(2.0 / math.pi)
GELU_B = 0.044715


def feed_kernel(narrow, own_rows, me_ref, x_ref, attn_ref, cot_ref, pad_ref, gb_ref, vec_ref, bup_ref, out_ref, dfirst_ref, dattn_ref, *refs):
    pieces, scratch = refs[: 2 * PIECES], refs[2 * PIECES :]
    act_ref, slope_ref, up_acc, down_acc, wo_acc, wo_low, side_ref, gv_ref, gbu_ref, sem = scratch
    step = pl.program_id(0)

    @pl.when(step == 0)
    def _():
        up_acc[...] = jnp.zeros_like(up_acc)
        down_acc[...] = jnp.zeros_like(down_acc)
        wo_acc[...] = jnp.zeros_like(wo_acc)
        gv_ref[...] = jnp.zeros_like(gv_ref)
        gbu_ref[...] = jnp.zeros_like(gbu_ref)

    gain_one, gain_two = vec_ref[3:4], vec_ref[6:7]
    keep_all = jnp.transpose(jnp.broadcast_to(pad_ref[...].astype(F32), (8, TILE)))[:, 0:1]
    parts = [slice(at, at + TILE // PARTS) for at in range(0, TILE, TILE // PARTS)]
    hidden, norm_one, r_one, hidden_t = {}, {}, {}, {}
    d_second, d_ff_t, d_hidden, d_branch_t, ff = {}, {}, {}, {}, {}

    def enter(p):
        rows = parts[p]
        first_sum = x_ref[rows].astype(F32) + (nt(attn_ref[rows], gb_ref[:, 0:D]) + vec_ref[2:3])
        norm_one[p], r_one[p] = centre(first_sum)
        hidden[p] = gain_one * norm_one[p] + vec_ref[4:5]

    def ahead(p):
        rows = parts[p]
        hidden_low = hidden[p].astype(BF)
        hidden_t[p] = jnp.transpose(hidden_low)
        ff[p] = 0.0
        for start, size in FF_CHUNKS:
            cols = slice(start, start + size)
            u = nn(hidden_low, gb_ref[:, D + start : D + start + size]) + bup_ref[0:1, cols]
            u2 = u * u
            t = jnp.tanh(u * (GELU_A + GELU_A * GELU_B * u2))
            h = 0.5 + 0.5 * t
            act = (u * h).astype(BF)
            act_ref[rows, cols] = act
            slope_ref[rows, cols] = (h + (u * h) * (1.0 - t) * (GELU_A + 3.0 * GELU_A * GELU_B * u2)).astype(BF)
            ff[p] = ff[p] + nt(act, gb_ref[:, D + FF + start : D + FF + start + size])

    def turn(p):
        rows = parts[p]
        keep = keep_all[rows]
        norm_two, r_two = centre(hidden[p] + (ff[p] + vec_ref[5:6]))
        out_ref[rows] = ((gain_two * norm_two + vec_ref[7:8]) * keep).astype(BF)
        top = cot_ref[rows].astype(F32) * keep
        gv_ref[6:7] += col_sum(top * norm_two)
        gv_ref[7:8] += col_sum(top)
        d_second[p] = norm_back(top * gain_two, norm_two, r_two)

    def behind(p):
        rows = parts[p]
        d_ff = d_second[p].astype(BF)
        gv_ref[5:6] += col_sum(d_ff.astype(F32))
        d_ff_t[p] = jnp.transpose(d_ff)
        d_hidden[p] = d_second[p]
        for start, size in FF_CHUNKS:
            cols = slice(start, start + size)
            d_act = nn(d_ff, gb_ref[:, D + FF + start : D + FF + start + size])
            d_pre = (slope_ref[rows, cols].astype(F32) * d_act).astype(BF)
            slope_ref[rows, cols] = d_pre
            gbu_ref[0:1, cols] += col_sum(d_pre.astype(F32))
            d_hidden[p] = d_hidden[p] + nt(d_pre, gb_ref[:, D + start : D + start + size])

    def leave(p):
        rows = parts[p]
        gv_ref[3:4] += col_sum(d_hidden[p] * norm_one[p])
        gv_ref[4:5] += col_sum(d_hidden[p])
        d_first = norm_back(d_hidden[p] * gain_one, norm_one[p], r_one[p])
        dfirst_ref[rows] = d_first
        d_branch = d_first.astype(BF)
        gv_ref[2:3] += col_sum(d_branch.astype(F32))
        d_branch_t[p] = jnp.transpose(d_branch)
        dattn_ref[rows] = nn(d_branch, gb_ref[:, 0:D]).astype(BF)

    def joined(pieces):
        return jnp.concatenate([pieces[p] for p in range(PARTS)], axis=1)

    def weights():
        ff_t, low_t = joined(d_ff_t), joined(hidden_t)
        for start, size in FF_CHUNKS:
            cols = slice(start, start + size)
            down_acc[:, cols] += nn(ff_t, act_ref[:, cols])
            up_acc[:, cols] += nn(low_t, slope_ref[:, cols])

    enter(0); ahead(0); turn(0); behind(0); leave(0); weights()
    wo_acc[...] += nn(joined(d_branch_t), attn_ref[...])

    @pl.when(step == pl.num_programs(0) - 1)
    def _():
        def send(ref, at, size):
            copies = block_copies(me_ref, ref, at, size, pieces, sem)
            for copy in copies:
                copy.start()
            return copies

        act_ref[...] = up_acc[...].astype(BF)
        copies = send(act_ref, D, FF)
        slope_ref[...] = down_acc[...].astype(BF)
        copies += send(slope_ref, D + FF, FF)
        wo_low[...] = wo_acc[...].astype(BF)
        copies += send(wo_low, 0, D)
        side = side_columns(narrow, own_rows, gbu_ref, side_ref.shape[1])
        vectors = jnp.transpose(jnp.concatenate([gv_ref[...], jnp.zeros((120, D), F32)], axis=0))
        first = side[:, 0:128] + vectors
        side_ref[:, 0:128] = first.astype(BF)
        if side_ref.shape[1] > 128:
            side_ref[:, 128:] = side[:, 128:].astype(BF)
        copies += send(side_ref, WB, side_ref.shape[1])
        for copy in copies:
            copy.wait()


def side_columns(narrow, own_rows, sums_ref, width):
    span = sums_ref.shape[1]
    bias = FF // narrow
    lane = lax.broadcasted_iota(jnp.int32, (1, width), 1)
    lines = []
    for n in range(narrow):
        for r in range(own_rows):
            at = r * (width - 8)
            if at < bias:
                moved = pltpu.roll(sums_ref[...], (span + 8 - n * bias - at) % span, 1)[0:1, 0:width]
                lines.append(jnp.where((lane >= 8) & (lane - 8 + at < bias), moved, 0.0))
            else:
                lines.append(jnp.zeros((1, width), F32))
    block = jnp.concatenate(lines, axis=0)
    return jnp.concatenate([block] * (D // block.shape[0]), axis=0)


def side_width(narrow, own_rows):
    return -(-(8 + -(-(FF // narrow) // own_rows)) // 128) * 128


def feed(narrow, own_rows, where, x, attn, cot, pad, gb, vec, bup):
    tokens = x.shape[0]
    side = side_width(narrow, own_rows)
    return pl.pallas_call(
        functools.partial(feed_kernel, narrow, own_rows),
        grid=(tokens // TILE,),
        in_specs=[
            SCALAR,
            rows_of(TILE, D),
            rows_of(TILE, D),
            rows_of(TILE, D),
            pl.BlockSpec((1, TILE), lambda i: (0, i)),
            whole((D, WB)),
            whole((128, D)),
            whole((1, FF)),
        ],
        out_specs=[rows_of(TILE, D), rows_of(TILE, D), rows_of(TILE, D)] + [LOOSE] * (2 * PIECES),
        out_shape=[
            jax.ShapeDtypeStruct((tokens, D), BF),
            jax.ShapeDtypeStruct((tokens, D), F32),
            jax.ShapeDtypeStruct((tokens, D), BF),
        ]
        + [jax.ShapeDtypeStruct((PIECE, WB + side), BF)] * (2 * PIECES),
        scratch_shapes=[
            pltpu.VMEM((TILE, FF), BF),
            pltpu.VMEM((TILE, FF), BF),
            pltpu.VMEM((D, FF), F32),
            pltpu.VMEM((D, FF), F32),
            pltpu.VMEM((D, D), F32),
            pltpu.VMEM((D, D), BF),
            pltpu.VMEM((D, side), BF),
            pltpu.VMEM((8, D), F32),
            pltpu.VMEM((8, FF + 128), F32),
            pltpu.SemaphoreType.DMA,
        ],
        compiler_params=pltpu.CompilerParams(vmem_limit_bytes=VMEM),
        cost_estimate=pl.CostEstimate(flops=80 * 10**9, bytes_accessed=40 * 10**6, transcendentals=0),
        name="feed",
    )(where, x, attn, cot, pad.reshape(1, tokens), gb, vec, bup)


def tn(a, b):
    return lax.dot_general(a, b, (((0,), (0,)), ((), ())), preferred_element_type=F32)


ACC = 3 * D + 2 * PLACES + 128


def core_kernel(me_ref, starts_ref, q_ref, k_ref, v_ref, dattn_ref, pt_ref, x_ref, mix_ref, picks_ref, al_ref, ar_ref, *refs):
    dq_ref, dk_ref, dv_ref, *pieces, acc, ga_ref, gw_ref, sem = refs[-(3 + 2 * PIECES + 4) :]
    step = pl.program_id(0)

    @pl.when(step == 0)
    def _():
        acc[...] = jnp.zeros_like(acc)

    for ref in (dq_ref, dk_ref, dv_ref):
        ref[...] = jnp.zeros_like(ref)

    def item(key_span, query_span, store):
        key_rows = key_span[1]
        queries, query_rows = query_span[:2]
        d_outs = [by_head(dattn_ref[query_rows, lanes]) for lanes in GROUP_LANES]
        d_probs = [nt(v_ref[key_rows, lanes], d_outs[g]) for g, lanes in enumerate(GROUP_LANES)]
        probs = [pt_ref[0, g, store, 0 : GROUP * queries] for g in range(GROUPS)]
        d_scores = []
        for g in range(GROUPS):
            wide = probs[g].astype(F32)
            delta = jnp.sum(wide * d_probs[g], axis=0, keepdims=True)
            d_scores.append((wide * (d_probs[g] - delta)).astype(BF))
        for g, lanes in enumerate(GROUP_LANES):
            dv_ref[key_rows, lanes] += nn(probs[g], d_outs[g]).astype(BF)
            dk_ref[key_rows, lanes] += nn(d_scores[g], by_head(q_ref[query_rows, lanes])).astype(BF)
            d_queries = heads_turned(jnp.transpose(k_ref[key_rows, lanes]), d_scores[g], queries) * SCALE
            dq_ref[query_rows, lanes] += jnp.transpose(d_queries.astype(BF))

    each_item(starts_ref, step, item)
    dq_t, dk_t, dv_t = (jnp.transpose(ref[...]) for ref in (dq_ref, dk_ref, dv_ref))
    mixed, picks = mix_ref[...], picks_ref[...]
    acc[:, 0:D] += nn(dq_t, mixed)
    acc[:, D : 2 * D] += nn(dk_t, mixed)
    acc[:, 2 * D : 3 * D] += nn(dv_t, x_ref[...])
    acc[:, 3 * D : 3 * D + PLACES] += nn(dq_t, picks)
    acc[:, 3 * D + PLACES : 3 * D + 2 * PLACES] += nn(dk_t, picks)
    acc[:, 3 * D + 2 * PLACES :] += nn(dv_t, jnp.ones((PACK, 128), BF))

    @pl.when(step == pl.num_programs(0) - 1)
    def _():
        load_blocks(me_ref, (al_ref, ar_ref), ga_ref, sem)
        gw_ref[:, 0 : 3 * D] = acc[:, 0 : 3 * D].astype(BF)
        table = tn(ga_ref[:, 0:D], acc[:, 3 * D : 3 * D + PLACES].astype(BF))
        table = table + tn(ga_ref[:, D : 2 * D], acc[:, 3 * D + PLACES : 3 * D + 2 * PLACES].astype(BF))
        gw_ref[:, 3 * D : WT] = table.astype(BF)
        lane = lax.broadcasted_iota(jnp.int32, (D, 128), 1)
        query_sum = acc[:, 3 * D + PLACES - 1 : 3 * D + PLACES]
        sums = jnp.where(lane == 0, query_sum, jnp.where(lane == 1, acc[:, 3 * D + 2 * PLACES :], 0.0))
        gw_ref[:, WT:] = sums.astype(BF)
        store_blocks(me_ref, gw_ref, pieces, sem)


def core_back(where, starts, q, k, v, d_attn, pt, x, mixed, picks, halves, after):
    tokens = x.shape[0]
    probs = pl.BlockSpec((1, GROUPS, PROB_ROWS, PROB_COLS), lambda i: (i, 0, 0, 0))
    flat = rows_of(PACK, D)
    return pl.pallas_call(
        core_kernel,
        grid=(tokens // PACK,),
        in_specs=[SCALAR, SCALAR] + [flat] * 4 + [probs, flat, flat, rows_of(PACK, PLACES)] + [LOOSE] * (2 + len(after)),
        out_specs=[flat] * 3 + [LOOSE] * (2 * PIECES),
        out_shape=[jax.ShapeDtypeStruct((tokens, D), BF)] * 3 + [jax.ShapeDtypeStruct((PIECE, WA), BF)] * (2 * PIECES),
        scratch_shapes=[pltpu.VMEM((D, ACC), F32), pltpu.VMEM((D, WA), BF), pltpu.VMEM((D, WA), BF), pltpu.SemaphoreType.DMA],
        compiler_params=pltpu.CompilerParams(vmem_limit_bytes=VMEM),
        cost_estimate=pl.CostEstimate(flops=50 * 10**9, bytes_accessed=50 * 10**6, transcendentals=0),
        name="core_back",
    )(where, starts, q, k, v, d_attn, pt, x, mixed, picks, *halves, *after)


def inputs_kernel(me_ref, dq_ref, dk_ref, dv_ref, dfirst_ref, al_ref, ar_ref, *refs):
    out_ref, ga_ref, sem = refs[-3:]

    @pl.when(pl.program_id(0) == 0)
    def _():
        load_blocks(me_ref, (al_ref, ar_ref), ga_ref, sem)

    d_mixed = nn(dq_ref[...], ga_ref[:, 0:D]) + nn(dk_ref[...], ga_ref[:, D : 2 * D])
    out_ref[...] = (dfirst_ref[...] + d_mixed + nn(dv_ref[...], ga_ref[:, 2 * D : 3 * D])).astype(BF)


def input_grads(where, flat, d_first, halves, after):
    tokens = d_first.shape[0]
    return pl.pallas_call(
        inputs_kernel,
        grid=(tokens // PACK,),
        in_specs=[SCALAR] + [rows_of(PACK, D)] * 4 + [LOOSE] * (2 + len(after)),
        out_specs=rows_of(PACK, D),
        out_shape=jax.ShapeDtypeStruct((tokens, D), BF),
        scratch_shapes=[pltpu.VMEM((D, WA), BF), pltpu.SemaphoreType.DMA],
        compiler_params=pltpu.CompilerParams(vmem_limit_bytes=VMEM),
        cost_estimate=pl.CostEstimate(flops=8 * 10**9, bytes_accessed=20 * 10**6, transcendentals=0),
        name="input_grads",
    )(where, *flat, d_first, *halves, *after)


def finish_kernel(count, *refs):
    a_refs, b_refs, outs, turn_ref = refs[:count], refs[count : 2 * count], refs[2 * count : -1], refs[-1]

    def total(pieces, start, size):
        result = pieces[0][:, start : start + size].astype(F32)
        for piece in pieces[1:]:
            result = result + piece[:, start : start + size].astype(F32)
        return result

    query, key, value, out, up, down, table = outs[:7]
    for at, ref in enumerate((query, key, value)):
        ref[...] = total(a_refs, at * D, D)
    out[...] = total(b_refs, 0, D)
    up[...] = total(b_refs, D, FF)
    down[...] = total(b_refs, D + FF, FF)
    table[...] = total(a_refs, 3 * D, PLACES)[:, 0:LONG]
    rows = query.shape[0]
    side = total(b_refs, WB, outs[-1].shape[1])
    outs[-1][...] = side
    lane = lax.broadcasted_iota(jnp.int32, (rows, 128), 1)
    turn_ref[...] = jnp.zeros_like(turn_ref)
    turn_ref[0:rows] = jnp.where(lane < 2, total(a_refs, WT, 128), side[:, 0:128])
    turned = jnp.transpose(turn_ref[...])
    for n, ref in enumerate(outs[7:15]):
        ref[...] = turned[n : n + 1, 0:rows]


def finish(a_parts, b_parts):
    rows = a_parts[0].shape[0]
    widths = [D, D, D, D, FF, FF, LONG]
    shapes = [(rows, width) for width in widths] + [(1, rows)] * 8 + [(rows, b_parts[0].shape[1] - WB)]
    vmem = pl.BlockSpec(memory_space=pltpu.VMEM)
    outs = pl.pallas_call(
        functools.partial(finish_kernel, len(a_parts)),
        in_specs=[vmem] * (2 * len(a_parts)),
        out_specs=[vmem] * len(shapes),
        out_shape=[jax.ShapeDtypeStruct(shape, F32) for shape in shapes],
        scratch_shapes=[pltpu.VMEM((128, 128), F32)],
        name="finish",
    )(*a_parts, *b_parts)
    return (*outs[:7], outs[7:15], outs[15])


def sines():
    half = D // 2
    frequency = np.exp(np.arange(half, dtype=np.float32) * np.float32(-2.0 * math.log(10000.0) / D))
    angles = frequency[:, None] * np.arange(PLACES, dtype=np.float32)[None, :]
    return jnp.asarray(np.concatenate([np.sin(angles), np.cos(angles)], axis=0).astype(np.float32))


def pack_kernel(piece, wide_ref, wq_ref, wk_ref, wv_ref, table_ref, wo_ref, up_ref, down_ref, bup_ref, *refs):
    vectors, (a_ref, b_ref, turn_ref, bias_ref) = refs[:8], refs[8:]
    rows = a_ref.shape[0]
    a_ref[:, 0:D] = wq_ref[...]
    a_ref[:, D : 2 * D] = wk_ref[...]
    a_ref[:, 2 * D : 3 * D] = wv_ref[...]
    a_ref[:, 3 * D : WT] = jnp.zeros((rows, PLACES), BF)
    a_ref[:, 3 * D : 3 * D + LONG] = table_ref[...]
    b_ref[:, 0:D] = wo_ref[...]
    b_ref[:, D : D + FF] = up_ref[...]
    b_ref[:, D + FF :] = down_ref[...]
    turn_ref[...] = jnp.zeros_like(turn_ref)
    for n, vector in enumerate(vectors):
        turn_ref[n : n + 1, 0:rows] = vector[...].astype(F32)
    bias_ref[...] = jnp.zeros_like(bias_ref)
    bias_ref[0:1, 0 : bup_ref.shape[1]] = bup_ref[...].astype(F32)
    span = bias_ref.shape[1]
    shift = lax.rem(span + 8 - wide_ref[0] * piece, span)
    moved = pltpu.roll(bias_ref[...], shift, 1)[0:1, 0:128]
    lane = lax.broadcasted_iota(jnp.int32, (rows, 128), 1)
    row = lax.broadcasted_iota(jnp.int32, (rows, 128), 0)
    mine = (row == 0) & (lane >= 8) & (lane < 8 + piece)
    columns = jnp.transpose(turn_ref[...])[0:rows]
    a_ref[:, WT:] = jnp.where(mine, moved, columns).astype(BF)


def pack(wide_index, piece, matrices, b_up, vectors):
    rows = matrices[0].shape[0]
    span = -(-(b_up.shape[0] + 8) // 128) * 128
    return pl.pallas_call(
        functools.partial(pack_kernel, piece),
        in_specs=[SCALAR] + [pl.BlockSpec(memory_space=pltpu.VMEM)] * 16,
        out_specs=[pl.BlockSpec(memory_space=pltpu.VMEM)] * 2,
        out_shape=[jax.ShapeDtypeStruct((rows, WA), BF), jax.ShapeDtypeStruct((rows, WB), BF)],
        scratch_shapes=[pltpu.VMEM((128, 128), F32), pltpu.VMEM((8, span), F32)],
        name="pack",
    )(wide_index.reshape(1), *matrices, b_up.reshape(1, -1), *[vector.reshape(1, rows) for vector in vectors])


def bit_groups(count):
    bits = count.bit_length() - 1
    return [(0,)] + [tuple(range(at, min(at + 2, bits))) for at in range(1, bits, 2)]


def offsets(count):
    found = [0]
    for group in bit_groups(count):
        found = [old | mask for old in found for mask in masks(group)]
    return found


def masks(group):
    return [index << group[0] for index in range(1 << len(group))]


def swap(block, mask, count):
    return lax.ppermute(block, AXES, [(i, i ^ mask) for i in range(count)])


def gather_phase(own, group, count):
    return [own] + [swap(own, mask, count) for mask in masks(group)[1:]]


def split_rows(block, count):
    rows = block.shape[0] // count
    return [block[at * rows : (at + 1) * rows] for at in range(count)]


def added(sources, parts):
    return split_rows(sum(source.astype(F32) for source in sources).astype(BF), parts)


def combine_kernel(count, parts, loose, *refs):
    sources, outs = refs[:count], refs[count + loose : count + loose + parts]
    total = sources[0][...].astype(F32)
    for source in sources[1:]:
        total = total + source[...].astype(F32)
    for n, out in enumerate(outs):

        @pl.when(pl.program_id(0) == n)
        def _(out=out):
            out[...] = total.astype(BF)


def combine(sources, parts, after=(), through=()):
    rows, width = sources[0].shape
    rows //= parts
    if rows % BLOCK:
        return added(sources, parts) + list(through)
    return list(pl.pallas_call(
        functools.partial(combine_kernel, len(sources), parts, len(after) + len(through)),
        grid=(parts,),
        in_specs=[rows_of(rows, width)] * len(sources) + [LOOSE] * (len(after) + len(through)),
        out_specs=[pl.BlockSpec((rows, width), lambda i: (0, 0), pipeline_mode=pl.Buffered(1))] * parts + [LOOSE] * len(through),
        out_shape=[jax.ShapeDtypeStruct((rows, width), BF)] * parts + [jax.ShapeDtypeStruct(array.shape, array.dtype) for array in through],
        input_output_aliases={len(sources) + len(after) + n: parts + n for n in range(len(through))},
        compiler_params=pltpu.CompilerParams(vmem_limit_bytes=VMEM),
        cost_estimate=pl.CostEstimate(flops=10**6, bytes_accessed=sum(2 * source.size * 2 for source in sources), transcendentals=0),
        name="combine",
    )(*sources, *after, *through))


def exchange(parts, group, count):
    return [parts[0]] + [swap(part, mask, count) for part, mask in zip(parts[1:], masks(group)[1:])]


def scatter_core(pieces, count):
    pairs = list(zip(pieces[:PIECES], pieces[PIECES:]))
    sums = [None] * PIECES
    for n in (1, 2, 3, 0):
        keep, send = pairs[n]
        sums[n] = (keep.astype(F32) + swap(send, 1, count).astype(F32)).astype(BF)
    return sums


def local(
    inputs,
    segments,
    pad_mask,
    cotangent,
    w_query,
    b_query,
    w_key,
    w_value,
    b_value,
    w_out,
    b_out,
    gain_one,
    shift_one,
    w_up,
    b_up,
    w_down,
    b_down,
    gain_two,
    shift_two,
    pos_table,
):
    tokens = inputs.shape[0]
    narrow = lax.axis_size("narrow")
    wide = lax.axis_size("wide")
    count = wide * narrow
    me = lax.axis_index(AXES)
    groups = bit_groups(count)
    own_rows = D // count
    bits = count.bit_length() - 1
    places = [bits - 1 - bit for group in groups for bit in reversed(group)] + [bits, bits + 1]
    in_kernel = own_rows == BLOCK
    where = (me if in_kernel else jnp.zeros((), jnp.int32)).reshape(1).astype(jnp.int32)

    def flips(full):
        for axis in range(bits):
            mine = (me >> (bits - 1 - axis)) & 1
            full = jnp.where(mine == 1, jnp.flip(full, axis), full)
        return full

    def absolute(halves):
        if in_kernel:
            return halves
        full = jnp.concatenate(halves, axis=0).reshape([2] * bits + [own_rows, -1])
        full = flips(full.transpose([places.index(axis) for axis in range(bits + 2)])).reshape(D, -1)
        return full[: D // 2], full[D // 2 :]

    def relative(pieces):
        if in_kernel:
            return pieces
        full = flips(jnp.concatenate(pieces, axis=0).reshape([2] * bits + [own_rows, -1]))
        return split_rows(full.transpose(places).reshape(D, -1), 2 * PIECES)

    seg = segments.reshape(1, tokens)
    packs = tokens // PACK
    below = segments.reshape(packs, 1, PACK) < jnp.arange(ITEMS + 1, dtype=jnp.int32)[None, :, None]
    starts = jnp.sum(below.astype(jnp.int32), axis=2).reshape(packs * (ITEMS + 1))
    bias_width = b_up.shape[0]
    bias_piece = -(-bias_width // wide)
    own_a, own_b = pack(
        lax.axis_index("wide").astype(jnp.int32),
        bias_piece,
        (w_query.T, w_key.T, w_value.T, pos_table.T, w_out.T, w_up, w_down.T),
        b_up,
        (b_query, b_value, b_out, gain_one, shift_one, b_down, gain_two, shift_two),
    )
    gb = lax.all_gather(own_b, AXES, axis=0, tiled=True)
    for group in reversed(groups[1:]):
        own_a = jnp.concatenate(gather_phase(own_a, group, count), axis=0)
    a_halves = absolute(tuple(gather_phase(own_a, groups[0], count)))
    q, k, v, mixed, attn, picks, pt, vec, pieces = attend(where, starts, seg, inputs, a_halves, sines())
    bup = pieces.reshape(wide, narrow, own_rows, 128)[:, :, 0, 8 : 8 + bias_piece].transpose(1, 0, 2)
    bup = bup.reshape(narrow, wide * bias_piece)[:, :bias_width].reshape(1, FF)
    layer_out, d_first, d_attn, *grads_b = feed(narrow, own_rows, where, inputs, attn, cotangent, pad_mask, gb, vec, bup)
    parts_b = scatter_core(relative(grads_b), count)
    back = core_back(where, starts, q, k, v, d_attn, pt, inputs, mixed, picks, a_halves, parts_b)
    grads_a = relative(back[3:])
    next_parts = 1 << len(groups[2])
    parts_b = combine(exchange(parts_b, groups[1], count), next_parts, (), grads_a[PIECES:])
    grads_a = [*grads_a[:PIECES], *parts_b[next_parts:]]
    parts_b = parts_b[:next_parts]
    parts_a = scatter_core(grads_a, count)
    input_grad = input_grads(where, back[:3], d_first, a_halves, parts_a + parts_b)
    parts_a = combine(exchange(parts_a, groups[1], count), 1 << len(groups[2]), [input_grad])
    for at in range(2, len(groups) - 1):
        next_parts = 1 << len(groups[at + 1])
        parts_b = added(exchange(parts_b, groups[at], count), next_parts)
        parts_a = added(exchange(parts_a, groups[at], count), next_parts)
    g_query, g_key, g_value, g_out, g_up, g_down, g_table, vectors, side = finish(
        exchange(parts_a, groups[-1], count), exchange(parts_b, groups[-1], count)
    )
    vectors = [vector.reshape(own_rows) for vector in vectors]
    grad_b_up = side[:, 8:].reshape(-1)[:bias_width]
    return (
        layer_out,
        input_grad,
        g_query.T,
        vectors[0],
        g_key.T,
        g_value.T,
        vectors[1],
        g_out.T,
        vectors[2],
        vectors[3],
        vectors[4],
        g_up,
        grad_b_up,
        g_down.T,
        vectors[5],
        vectors[6],
        vectors[7],
        g_table.T,
    )


def solution(mesh):
    both = P(("wide", "narrow"))
    rows = P(("wide", "narrow"), None)
    cols = P(None, ("wide", "narrow"))
    in_specs = (rows, both, both, rows, cols, both, cols, cols, both, cols, both, both, both, rows, P("narrow"), cols, both, both, both, cols)
    out_specs = (rows, rows, cols, both, cols, cols, both, cols, both, both, both, rows, P("narrow"), cols, both, both, both, cols)
    return jax.shard_map(local, mesh=mesh, in_specs=in_specs, out_specs=out_specs, check_vma=False)
```

```python
import functools
import math

import jax
import jax.numpy as jnp
import numpy as np
from jax import lax
from jax.experimental import pallas as pl
from jax.experimental.pallas import tpu as pltpu
from jax.sharding import PartitionSpec as P

D = 512
H = 8
FF = 3200
HD = 64
PACK = 640
LONG = 302
PLACES = 384
SCALE = 0.125
EPS = 1e-05
NEG = -1e9
WT = 3 * D + PLACES
WA = WT + 128
BLOCK = 16
BLOCKS = D // BLOCK
PIECES = 4
PIECE = D // (2 * PIECES)
WB = D + 2 * FF
TILE = 512
PARTS = 1
FF_CHUNKS = ((0, 1536), (1536, 1664))
ITEMS = 9
SHORT_WINDOW = (96, 128)
LONG_WINDOW = (320, 384)
SHORT_MOST = SHORT_WINDOW[0] - 15
PROB_ROWS = 1024
GROUP = 4
GROUPS = H // GROUP
GD = GROUP * HD
PROB_COLS = GROUP * LONG_WINDOW[1]
AXES = ("wide", "narrow")
VMEM = 60 * 1024 * 1024
BF = jnp.bfloat16
F32 = jnp.float32


def nn(a, b):
    return lax.dot_general(a, b, (((1,), (0,)), ((), ())), preferred_element_type=F32)


def nt(a, b):
    return lax.dot_general(a, b, (((1,), (1,)), ((), ())), preferred_element_type=F32)


def item_masks(seg_row):
    wide = jnp.broadcast_to(seg_row.astype(F32), (8, PACK))
    col = jnp.transpose(wide)[:, 0:1]
    return col == wide[0:1]


def place_picks(same):
    lane = lax.broadcasted_iota(jnp.int32, (PACK, PACK), 1).astype(F32)
    first = jnp.min(jnp.where(same, lane, 1e6), axis=1, keepdims=True)
    place = lax.broadcasted_iota(jnp.int32, (PACK, 1), 0).astype(F32) - first
    slot = lax.broadcasted_iota(jnp.int32, (PACK, PLACES), 1).astype(F32)
    return jnp.where((place == slot) | (slot == PLACES - 1), 1.0, 0.0).astype(BF)


def each_item(starts_ref, pack, body):
    def visit(n, place):
        first = starts_ref[pack * (ITEMS + 1) + n]
        end = starts_ref[pack * (ITEMS + 1) + n + 1]
        length = end - first

        def window(sizes):
            spans = []
            for size in sizes:
                base = pl.multiple_of(jnp.minimum(lax.div(first, 16) * 16, PACK - size), 16)
                spans.append((size, pl.ds(base, size), first - base, end - base))
            body(*spans, pl.ds(pl.multiple_of(place, 16), sizes[0]))

        short = length <= SHORT_MOST

        @pl.when((length > 0) & short)
        def _():
            window(SHORT_WINDOW)

        @pl.when(length > SHORT_MOST)
        def _():
            window(LONG_WINDOW)

        return place + jnp.where(length > 0, jnp.where(short, SHORT_WINDOW[0], LONG_WINDOW[0]), 0)

    lax.fori_loop(0, ITEMS, visit, jnp.int32(0))


def by_head(block):
    lane = lax.broadcasted_iota(jnp.int32, block.shape, 1)
    zero = jnp.zeros_like(block)
    return jnp.concatenate([jnp.where((lane >= h * HD) & (lane < (h + 1) * HD), block, zero) for h in range(GROUP)], axis=0)


def heads_turned(left_t, right, size):
    parts = [nn(left_t[h * HD : (h + 1) * HD], right[:, h * size : (h + 1) * size]) for h in range(GROUP)]
    return jnp.concatenate(parts, axis=0)


GROUP_LANES = [slice(g * GD, (g + 1) * GD) for g in range(GROUPS)]


def block_rows(me_ref, place):
    owner = me_ref[0] ^ offsets(BLOCKS)[place]
    return pl.ds(pl.multiple_of(owner * BLOCK, BLOCK), BLOCK)


def block_loads(me_ref, halves, full_ref, sem):
    copies = []
    for place in range(BLOCKS):
        half, at = divmod(place, BLOCKS // 2)
        copies.append(pltpu.make_async_copy(halves[half].at[at * BLOCK : (at + 1) * BLOCK], full_ref.at[block_rows(me_ref, place)], sem))
    return copies


def load_blocks(me_ref, halves, full_ref, sem):
    copies = block_loads(me_ref, halves, full_ref, sem)
    for copy in copies:
        copy.start()
    for copy in copies:
        copy.wait()


def block_copies(me_ref, ref, col, width, pieces, sem):
    copies = []
    for place in range(BLOCKS):
        piece, at = divmod(place * BLOCK, PIECE)
        target = pieces[piece].at[at : at + BLOCK, col : col + width]
        copies.append(pltpu.make_async_copy(ref.at[block_rows(me_ref, place)], target, sem))
    return copies


def store_blocks(me_ref, ref, pieces, sem):
    copies = block_copies(me_ref, ref, 0, ref.shape[1], pieces, sem)
    for copy in copies:
        copy.start()
    for copy in copies:
        copy.wait()


def attend_kernel(me_ref, starts_ref, seg_ref, x_ref, al_ref, ar_ref, st_ref, q_ref, k_ref, v_ref, mix_ref, attn_ref, picks_ref, pt_ref, vec_ref, pieces_ref, ga_ref, hi_ref, lo_ref, sem):
    @pl.when(pl.program_id(0) == 0)
    def _():
        load_blocks(me_ref, (al_ref, ar_ref), ga_ref, sem)
        pieces_ref[...] = ga_ref[:, WT:].astype(F32)
        vec_ref[...] = jnp.transpose(pieces_ref[...])
        pos = st_ref[...] + ga_ref[:, 3 * D : 3 * D + PLACES].astype(F32)
        pos = jnp.where(lax.broadcasted_iota(jnp.int32, pos.shape, 1) < LONG, pos, 0.0)
        hi = pos.astype(BF)
        hi_ref[...] = hi
        lo_ref[...] = (pos - hi.astype(F32)).astype(BF)

    picks = place_picks(item_masks(seg_ref[...]))
    picks_ref[...] = picks
    x = x_ref[...]
    positions = nt(picks, hi_ref[...]) + nt(picks, lo_ref[...])
    mixed = (x.astype(F32) + positions).astype(BF)
    mix_ref[...] = mixed
    q_ref[...] = ((nt(mixed, ga_ref[:, 0:D]) + vec_ref[0:1]).astype(BF).astype(F32) * SCALE).astype(BF)
    k_ref[...] = nt(mixed, ga_ref[:, D : 2 * D]).astype(BF)
    v = (nt(x, ga_ref[:, 2 * D : 3 * D]) + vec_ref[1:2]).astype(BF)
    v_ref[...] = v
    attn_ref[...] = jnp.zeros_like(attn_ref)

    def item(key_span, query_span, store):
        keys, key_rows, low, high = key_span
        down = lax.broadcasted_iota(jnp.int32, (keys, 1), 0)
        shut = jnp.where((down >= low) & (down < high), 0.0, NEG)
        queries, query_rows, low, high = query_span
        across = lax.broadcasted_iota(jnp.int32, (1, queries), 1)
        live = jnp.where((across >= low) & (across < high), 1.0, 0.0)
        live = jnp.concatenate([live] * GROUP, axis=1)
        scores = [nt(k_ref[key_rows, lanes], by_head(q_ref[query_rows, lanes])) + shut for lanes in GROUP_LANES]
        probs = []
        for g in range(GROUPS):
            exps = jnp.exp(scores[g] - jnp.max(scores[g], axis=0, keepdims=True))
            scale = live / jnp.sum(exps, axis=0, keepdims=True)
            probs.append((exps * scale).astype(BF))
            pt_ref[0, g, store, 0 : GROUP * queries] = probs[g]
        for g, lanes in enumerate(GROUP_LANES):
            outs = heads_turned(jnp.transpose(v_ref[key_rows, lanes]), probs[g], queries)
            attn_ref[query_rows, lanes] += jnp.transpose(outs.astype(BF))

    each_item(starts_ref, pl.program_id(0), item)


def whole(shape):
    return pl.BlockSpec(shape, lambda i: tuple(0 for _ in shape), pipeline_mode=pl.Buffered(1))


def rows_of(count, width):
    return pl.BlockSpec((count, width), lambda i: (i, 0))


SCALAR = pl.BlockSpec(memory_space=pltpu.SMEM)
LOOSE = pl.BlockSpec(memory_space=pl.ANY)


def attend(where, starts, seg, x, halves, st):
    tokens = seg.shape[1]
    packs = tokens // PACK
    low = jax.ShapeDtypeStruct((tokens, D), BF)
    return pl.pallas_call(
        attend_kernel,
        grid=(packs,),
        in_specs=[SCALAR, SCALAR, pl.BlockSpec((1, PACK), lambda i: (0, i)), rows_of(PACK, D), LOOSE, LOOSE, whole((D, PLACES))],
        out_specs=[rows_of(PACK, D)] * 5 + [rows_of(PACK, PLACES), pl.BlockSpec((1, GROUPS, PROB_ROWS, PROB_COLS), lambda i: (i, 0, 0, 0)), whole((128, D)), whole((D, 128))],
        out_shape=[low] * 5
        + [
            jax.ShapeDtypeStruct((tokens, PLACES), BF),
            jax.ShapeDtypeStruct((packs, GROUPS, PROB_ROWS, PROB_COLS), BF), jax.ShapeDtypeStruct((128, D), F32), jax.ShapeDtypeStruct((D, 128), F32)],
        scratch_shapes=[
            pltpu.VMEM((D, WA), BF),
            pltpu.VMEM((D, PLACES), BF),
            pltpu.VMEM((D, PLACES), BF),
            pltpu.SemaphoreType.DMA,
        ],
        compiler_params=pltpu.CompilerParams(vmem_limit_bytes=VMEM),
        cost_estimate=pl.CostEstimate(flops=40 * 10**9, bytes_accessed=50 * 10**6, transcendentals=0),
        name="attend",
    )(where, starts, seg, x, *halves, st)


def centre(v):
    c = v - jnp.mean(v, axis=-1, keepdims=True)
    r = lax.rsqrt(jnp.mean(c * c, axis=-1, keepdims=True) + EPS)
    return c * r, r


def norm_back(g, n, r):
    return r * (g - jnp.mean(g, axis=-1, keepdims=True) - n * jnp.mean(g * n, axis=-1, keepdims=True))


def col_sum(v):
    return jnp.sum(v, axis=0, keepdims=True)


GELU_A = math.sqrt(2.0 / math.pi)
GELU_B = 0.044715


def feed_kernel(narrow, own_rows, me_ref, x_ref, attn_ref, cot_ref, pad_ref, gb_hbm, vec_ref, bup_ref, out_ref, dfirst_ref, dattn_ref, *refs):
    pieces, scratch = refs[: 2 * PIECES], refs[2 * PIECES :]
    gb_ref, act_ref, slope_ref, up_acc, down_acc, wo_acc, wo_low, side_ref, gv_ref, gbu_ref, sem, load_sems = scratch
    loads = [
        pltpu.make_async_copy(gb_hbm.at[:, at : at + size], gb_ref.at[:, at : at + size], load_sems.at[n])
        for n, (at, size) in enumerate(((0, D), (D, FF), (D + FF, FF)))
    ]
    step = pl.program_id(0)

    @pl.when(step == 0)
    def _():
        for copy in loads:
            copy.start()
        up_acc[...] = jnp.zeros_like(up_acc)
        down_acc[...] = jnp.zeros_like(down_acc)
        wo_acc[...] = jnp.zeros_like(wo_acc)
        gv_ref[...] = jnp.zeros_like(gv_ref)
        gbu_ref[...] = jnp.zeros_like(gbu_ref)
        loads[0].wait()

    gain_one, gain_two = vec_ref[3:4], vec_ref[6:7]
    keep_all = jnp.transpose(jnp.broadcast_to(pad_ref[...].astype(F32), (8, TILE)))[:, 0:1]
    parts = [slice(at, at + TILE // PARTS) for at in range(0, TILE, TILE // PARTS)]
    hidden, norm_one, r_one, hidden_t = {}, {}, {}, {}
    d_second, d_ff_t, d_hidden, d_branch_t, ff = {}, {}, {}, {}, {}

    def enter(p):
        rows = parts[p]
        first_sum = x_ref[rows].astype(F32) + (nt(attn_ref[rows], gb_ref[:, 0:D]) + vec_ref[2:3])
        norm_one[p], r_one[p] = centre(first_sum)
        hidden[p] = gain_one * norm_one[p] + vec_ref[4:5]

    def ahead(p):
        rows = parts[p]
        hidden_low = hidden[p].astype(BF)
        hidden_t[p] = jnp.transpose(hidden_low)
        ff[p] = 0.0
        for start, size in FF_CHUNKS:
            cols = slice(start, start + size)
            u = nn(hidden_low, gb_ref[:, D + start : D + start + size]) + bup_ref[0:1, cols]
            u2 = u * u
            t = jnp.tanh(u * (GELU_A + GELU_A * GELU_B * u2))
            h = 0.5 + 0.5 * t
            act = (u * h).astype(BF)
            act_ref[rows, cols] = act
            slope_ref[rows, cols] = (h + (u * h) * (1.0 - t) * (GELU_A + 3.0 * GELU_A * GELU_B * u2)).astype(BF)
            ff[p] = ff[p] + nt(act, gb_ref[:, D + FF + start : D + FF + start + size])

    def turn(p):
        rows = parts[p]
        keep = keep_all[rows]
        norm_two, r_two = centre(hidden[p] + (ff[p] + vec_ref[5:6]))
        out_ref[rows] = ((gain_two * norm_two + vec_ref[7:8]) * keep).astype(BF)
        top = cot_ref[rows].astype(F32) * keep
        gv_ref[6:7] += col_sum(top * norm_two)
        gv_ref[7:8] += col_sum(top)
        d_second[p] = norm_back(top * gain_two, norm_two, r_two)

    def behind(p):
        rows = parts[p]
        d_ff = d_second[p].astype(BF)
        gv_ref[5:6] += col_sum(d_ff.astype(F32))
        d_ff_t[p] = jnp.transpose(d_ff)
        d_hidden[p] = d_second[p]
        for start, size in FF_CHUNKS:
            cols = slice(start, start + size)
            d_act = nn(d_ff, gb_ref[:, D + FF + start : D + FF + start + size])
            d_pre = (slope_ref[rows, cols].astype(F32) * d_act).astype(BF)
            slope_ref[rows, cols] = d_pre
            gbu_ref[0:1, cols] += col_sum(d_pre.astype(F32))
            d_hidden[p] = d_hidden[p] + nt(d_pre, gb_ref[:, D + start : D + start + size])

    def leave(p):
        rows = parts[p]
        gv_ref[3:4] += col_sum(d_hidden[p] * norm_one[p])
        gv_ref[4:5] += col_sum(d_hidden[p])
        d_first = norm_back(d_hidden[p] * gain_one, norm_one[p], r_one[p])
        dfirst_ref[rows] = d_first
        d_branch = d_first.astype(BF)
        gv_ref[2:3] += col_sum(d_branch.astype(F32))
        d_branch_t[p] = jnp.transpose(d_branch)
        dattn_ref[rows] = nn(d_branch, gb_ref[:, 0:D]).astype(BF)

    def joined(pieces):
        return jnp.concatenate([pieces[p] for p in range(PARTS)], axis=1)

    def weights():
        ff_t, low_t = joined(d_ff_t), joined(hidden_t)
        for start, size in FF_CHUNKS:
            cols = slice(start, start + size)
            down_acc[:, cols] += nn(ff_t, act_ref[:, cols])
            up_acc[:, cols] += nn(low_t, slope_ref[:, cols])

    enter(0)

    @pl.when(step == 0)
    def _():
        loads[1].wait()
        loads[2].wait()

    ahead(0)
    turn(0)
    behind(0)
    leave(0)
    weights()
    wo_acc[...] += nn(joined(d_branch_t), attn_ref[...])

    @pl.when(step == pl.num_programs(0) - 1)
    def _():
        def send(ref, at, size):
            copies = block_copies(me_ref, ref, at, size, pieces, sem)
            for copy in copies:
                copy.start()
            return copies

        act_ref[...] = up_acc[...].astype(BF)
        copies = send(act_ref, D, FF)
        slope_ref[...] = down_acc[...].astype(BF)
        copies += send(slope_ref, D + FF, FF)
        wo_low[...] = wo_acc[...].astype(BF)
        copies += send(wo_low, 0, D)
        side = side_columns(narrow, own_rows, gbu_ref, side_ref.shape[1])
        vectors = jnp.transpose(jnp.concatenate([gv_ref[...], jnp.zeros((120, D), F32)], axis=0))
        first = side[:, 0:128] + vectors
        side_ref[:, 0:128] = first.astype(BF)
        if side_ref.shape[1] > 128:
            side_ref[:, 128:] = side[:, 128:].astype(BF)
        copies += send(side_ref, WB, side_ref.shape[1])
        for copy in copies:
            copy.wait()


def side_columns(narrow, own_rows, sums_ref, width):
    span = sums_ref.shape[1]
    bias = FF // narrow
    lane = lax.broadcasted_iota(jnp.int32, (1, width), 1)
    lines = []
    for n in range(narrow):
        for r in range(own_rows):
            at = r * (width - 8)
            if at < bias:
                moved = pltpu.roll(sums_ref[...], (span + 8 - n * bias - at) % span, 1)[0:1, 0:width]
                lines.append(jnp.where((lane >= 8) & (lane - 8 + at < bias), moved, 0.0))
            else:
                lines.append(jnp.zeros((1, width), F32))
    block = jnp.concatenate(lines, axis=0)
    return jnp.concatenate([block] * (D // block.shape[0]), axis=0)


def side_width(narrow, own_rows):
    return -(-(8 + -(-(FF // narrow) // own_rows)) // 128) * 128


def feed(narrow, own_rows, where, x, attn, cot, pad, gb, vec, bup):
    tokens = x.shape[0]
    side = side_width(narrow, own_rows)
    return pl.pallas_call(
        functools.partial(feed_kernel, narrow, own_rows),
        grid=(tokens // TILE,),
        in_specs=[
            SCALAR,
            rows_of(TILE, D),
            rows_of(TILE, D),
            rows_of(TILE, D),
            pl.BlockSpec((1, TILE), lambda i: (0, i)),
            LOOSE,
            whole((128, D)),
            whole((1, FF)),
        ],
        out_specs=[rows_of(TILE, D), rows_of(TILE, D), rows_of(TILE, D)] + [LOOSE] * (2 * PIECES),
        out_shape=[
            jax.ShapeDtypeStruct((tokens, D), BF),
            jax.ShapeDtypeStruct((tokens, D), F32),
            jax.ShapeDtypeStruct((tokens, D), BF),
        ]
        + [jax.ShapeDtypeStruct((PIECE, WB + side), BF)] * (2 * PIECES),
        scratch_shapes=[
            pltpu.VMEM((D, WB), BF),
            pltpu.VMEM((TILE, FF), BF),
            pltpu.VMEM((TILE, FF), BF),
            pltpu.VMEM((D, FF), F32),
            pltpu.VMEM((D, FF), F32),
            pltpu.VMEM((D, D), F32),
            pltpu.VMEM((D, D), BF),
            pltpu.VMEM((D, side), BF),
            pltpu.VMEM((8, D), F32),
            pltpu.VMEM((8, FF + 128), F32),
            pltpu.SemaphoreType.DMA,
            pltpu.SemaphoreType.DMA((3,)),
        ],
        compiler_params=pltpu.CompilerParams(vmem_limit_bytes=VMEM),
        cost_estimate=pl.CostEstimate(flops=80 * 10**9, bytes_accessed=40 * 10**6, transcendentals=0),
        name="feed",
    )(where, x, attn, cot, pad.reshape(1, tokens), gb, vec, bup)


def tn(a, b):
    return lax.dot_general(a, b, (((0,), (0,)), ((), ())), preferred_element_type=F32)


ACC = 3 * D + 2 * PLACES + 128


def core_kernel(me_ref, starts_ref, q_ref, k_ref, v_ref, dattn_ref, pt_ref, x_ref, mix_ref, picks_ref, al_ref, ar_ref, *refs):
    dq_ref, dk_ref, dv_ref, *pieces, acc, ga_ref, gw_ref, sem, load_sem = refs[-(3 + 2 * PIECES + 5) :]
    step = pl.program_id(0)

    loads = block_loads(me_ref, (al_ref, ar_ref), ga_ref, load_sem)

    @pl.when(step == 0)
    def _():
        for copy in loads:
            copy.start()
        acc[...] = jnp.zeros_like(acc)

    for ref in (dq_ref, dk_ref, dv_ref):
        ref[...] = jnp.zeros_like(ref)

    def item(key_span, query_span, store):
        key_rows = key_span[1]
        queries, query_rows = query_span[:2]
        d_outs = [by_head(dattn_ref[query_rows, lanes]) for lanes in GROUP_LANES]
        d_probs = [nt(v_ref[key_rows, lanes], d_outs[g]) for g, lanes in enumerate(GROUP_LANES)]
        probs = [pt_ref[0, g, store, 0 : GROUP * queries] for g in range(GROUPS)]
        d_scores = []
        for g in range(GROUPS):
            wide = probs[g].astype(F32)
            delta = jnp.sum(wide * d_probs[g], axis=0, keepdims=True)
            d_scores.append((wide * (d_probs[g] - delta)).astype(BF))
        for g, lanes in enumerate(GROUP_LANES):
            dv_ref[key_rows, lanes] += nn(probs[g], d_outs[g]).astype(BF)
            dk_ref[key_rows, lanes] += nn(d_scores[g], by_head(q_ref[query_rows, lanes])).astype(BF)
            d_queries = heads_turned(jnp.transpose(k_ref[key_rows, lanes]), d_scores[g], queries) * SCALE
            dq_ref[query_rows, lanes] += jnp.transpose(d_queries.astype(BF))

    each_item(starts_ref, step, item)
    dq_t, dk_t, dv_t = (jnp.transpose(ref[...]) for ref in (dq_ref, dk_ref, dv_ref))
    mixed, picks = mix_ref[...], picks_ref[...]
    acc[:, 0:D] += nn(dq_t, mixed)
    acc[:, D : 2 * D] += nn(dk_t, mixed)
    acc[:, 2 * D : 3 * D] += nn(dv_t, x_ref[...])
    acc[:, 3 * D : 3 * D + PLACES] += nn(dq_t, picks)
    acc[:, 3 * D + PLACES : 3 * D + 2 * PLACES] += nn(dk_t, picks)
    acc[:, 3 * D + 2 * PLACES :] += nn(dv_t, jnp.ones((PACK, 128), BF))

    @pl.when(step == pl.num_programs(0) - 1)
    def _():
        for copy in loads:
            copy.wait()
        gw_ref[:, 0 : 3 * D] = acc[:, 0 : 3 * D].astype(BF)
        table = tn(ga_ref[:, 0:D], acc[:, 3 * D : 3 * D + PLACES].astype(BF))
        table = table + tn(ga_ref[:, D : 2 * D], acc[:, 3 * D + PLACES : 3 * D + 2 * PLACES].astype(BF))
        gw_ref[:, 3 * D : WT] = table.astype(BF)
        lane = lax.broadcasted_iota(jnp.int32, (D, 128), 1)
        query_sum = acc[:, 3 * D + PLACES - 1 : 3 * D + PLACES]
        sums = jnp.where(lane == 0, query_sum, jnp.where(lane == 1, acc[:, 3 * D + 2 * PLACES :], 0.0))
        gw_ref[:, WT:] = sums.astype(BF)
        store_blocks(me_ref, gw_ref, pieces, sem)


def core_back(where, starts, q, k, v, d_attn, pt, x, mixed, picks, halves, after):
    tokens = x.shape[0]
    probs = pl.BlockSpec((1, GROUPS, PROB_ROWS, PROB_COLS), lambda i: (i, 0, 0, 0))
    flat = rows_of(PACK, D)
    return pl.pallas_call(
        core_kernel,
        grid=(tokens // PACK,),
        in_specs=[SCALAR, SCALAR] + [flat] * 4 + [probs, flat, flat, rows_of(PACK, PLACES)] + [LOOSE] * (2 + len(after)),
        out_specs=[flat] * 3 + [LOOSE] * (2 * PIECES),
        out_shape=[jax.ShapeDtypeStruct((tokens, D), BF)] * 3 + [jax.ShapeDtypeStruct((PIECE, WA), BF)] * (2 * PIECES),
        scratch_shapes=[
            pltpu.VMEM((D, ACC), F32),
            pltpu.VMEM((D, WA), BF),
            pltpu.VMEM((D, WA), BF),
            pltpu.SemaphoreType.DMA,
            pltpu.SemaphoreType.DMA,
        ],
        compiler_params=pltpu.CompilerParams(vmem_limit_bytes=VMEM),
        cost_estimate=pl.CostEstimate(flops=50 * 10**9, bytes_accessed=50 * 10**6, transcendentals=0),
        name="core_back",
    )(where, starts, q, k, v, d_attn, pt, x, mixed, picks, *halves, *after)


def inputs_kernel(me_ref, dq_ref, dk_ref, dv_ref, dfirst_ref, al_ref, ar_ref, *refs):
    out_ref, _, ga_ref, sem = refs[-4:]

    @pl.when(pl.program_id(0) == 0)
    def _():
        load_blocks(me_ref, (al_ref, ar_ref), ga_ref, sem)

    d_mixed = nn(dq_ref[...], ga_ref[:, 0:D]) + nn(dk_ref[...], ga_ref[:, D : 2 * D])
    out_ref[...] = (dfirst_ref[...] + d_mixed + nn(dv_ref[...], ga_ref[:, 2 * D : 3 * D])).astype(BF)


def input_grads(where, flat, d_first, halves, after, through):
    tokens = d_first.shape[0]
    return pl.pallas_call(
        inputs_kernel,
        grid=(tokens // PACK,),
        in_specs=[SCALAR] + [rows_of(PACK, D)] * 4 + [LOOSE] * (3 + len(after)),
        out_specs=[rows_of(PACK, D), LOOSE],
        out_shape=[jax.ShapeDtypeStruct((tokens, D), BF), jax.ShapeDtypeStruct(through.shape, through.dtype)],
        input_output_aliases={7 + len(after): 1},
        scratch_shapes=[pltpu.VMEM((D, WA), BF), pltpu.SemaphoreType.DMA],
        compiler_params=pltpu.CompilerParams(vmem_limit_bytes=VMEM),
        cost_estimate=pl.CostEstimate(flops=8 * 10**9, bytes_accessed=20 * 10**6, transcendentals=0),
        name="input_grads",
    )(where, *flat, d_first, *halves, *after, through)


def finish_kernel(count, *refs):
    a_refs, b_refs, outs, turn_ref = refs[:count], refs[count : 2 * count], refs[2 * count : -1], refs[-1]

    def total(pieces, start, size):
        result = pieces[0][:, start : start + size].astype(F32)
        for piece in pieces[1:]:
            result = result + piece[:, start : start + size].astype(F32)
        return result

    query, key, value, out, up, down, table = outs[:7]
    for at, ref in enumerate((query, key, value)):
        ref[...] = total(a_refs, at * D, D)
    out[...] = total(b_refs, 0, D)
    up[...] = total(b_refs, D, FF)
    down[...] = total(b_refs, D + FF, FF)
    table[...] = total(a_refs, 3 * D, PLACES)[:, 0:LONG]
    rows = query.shape[0]
    side = total(b_refs, WB, outs[-1].shape[1])
    outs[-1][...] = side
    lane = lax.broadcasted_iota(jnp.int32, (rows, 128), 1)
    turn_ref[...] = jnp.zeros_like(turn_ref)
    turn_ref[0:rows] = jnp.where(lane < 2, total(a_refs, WT, 128), side[:, 0:128])
    turned = jnp.transpose(turn_ref[...])
    for n, ref in enumerate(outs[7:15]):
        ref[...] = turned[n : n + 1, 0:rows]


def finish(a_parts, b_parts):
    rows = a_parts[0].shape[0]
    widths = [D, D, D, D, FF, FF, LONG]
    shapes = [(rows, width) for width in widths] + [(1, rows)] * 8 + [(rows, b_parts[0].shape[1] - WB)]
    vmem = pl.BlockSpec(memory_space=pltpu.VMEM)
    outs = pl.pallas_call(
        functools.partial(finish_kernel, len(a_parts)),
        in_specs=[vmem] * (2 * len(a_parts)),
        out_specs=[vmem] * len(shapes),
        out_shape=[jax.ShapeDtypeStruct(shape, F32) for shape in shapes],
        scratch_shapes=[pltpu.VMEM((128, 128), F32)],
        name="finish",
    )(*a_parts, *b_parts)
    return (*outs[:7], outs[7:15], outs[15])


def sines():
    half = D // 2
    frequency = np.exp(np.arange(half, dtype=np.float32) * np.float32(-2.0 * math.log(10000.0) / D))
    angles = frequency[:, None] * np.arange(PLACES, dtype=np.float32)[None, :]
    return jnp.asarray(np.concatenate([np.sin(angles), np.cos(angles)], axis=0).astype(np.float32))


def pack_kernel(piece, wide_ref, wq_ref, wk_ref, wv_ref, table_ref, wo_ref, up_ref, down_ref, bup_ref, *refs):
    vectors, (a_ref, b_ref, turn_ref, bias_ref) = refs[:8], refs[8:]
    rows = a_ref.shape[0]
    a_ref[:, 0:D] = wq_ref[...]
    a_ref[:, D : 2 * D] = wk_ref[...]
    a_ref[:, 2 * D : 3 * D] = wv_ref[...]
    a_ref[:, 3 * D : WT] = jnp.zeros((rows, PLACES), BF)
    a_ref[:, 3 * D : 3 * D + LONG] = table_ref[...]
    b_ref[:, 0:D] = wo_ref[...]
    b_ref[:, D : D + FF] = up_ref[...]
    b_ref[:, D + FF :] = down_ref[...]
    turn_ref[...] = jnp.zeros_like(turn_ref)
    for n, vector in enumerate(vectors):
        turn_ref[n : n + 1, 0:rows] = vector[...].astype(F32)
    bias_ref[...] = jnp.zeros_like(bias_ref)
    bias_ref[0:1, 0 : bup_ref.shape[1]] = bup_ref[...].astype(F32)
    span = bias_ref.shape[1]
    shift = lax.rem(span + 8 - wide_ref[0] * piece, span)
    moved = pltpu.roll(bias_ref[...], shift, 1)[0:1, 0:128]
    lane = lax.broadcasted_iota(jnp.int32, (rows, 128), 1)
    row = lax.broadcasted_iota(jnp.int32, (rows, 128), 0)
    mine = (row == 0) & (lane >= 8) & (lane < 8 + piece)
    columns = jnp.transpose(turn_ref[...])[0:rows]
    a_ref[:, WT:] = jnp.where(mine, moved, columns).astype(BF)


def pack(wide_index, piece, matrices, b_up, vectors):
    rows = matrices[0].shape[0]
    span = -(-(b_up.shape[0] + 8) // 128) * 128
    return pl.pallas_call(
        functools.partial(pack_kernel, piece),
        in_specs=[SCALAR] + [pl.BlockSpec(memory_space=pltpu.VMEM)] * 16,
        out_specs=[pl.BlockSpec(memory_space=pltpu.VMEM)] * 2,
        out_shape=[jax.ShapeDtypeStruct((rows, WA), BF), jax.ShapeDtypeStruct((rows, WB), BF)],
        scratch_shapes=[pltpu.VMEM((128, 128), F32), pltpu.VMEM((8, span), F32)],
        name="pack",
    )(wide_index.reshape(1), *matrices, b_up.reshape(1, -1), *[vector.reshape(1, rows) for vector in vectors])


def bit_groups(count):
    bits = count.bit_length() - 1
    return [(0,)] + [tuple(range(at, min(at + 2, bits))) for at in range(1, bits, 2)]


def offsets(count):
    found = [0]
    for group in bit_groups(count):
        found = [old | mask for old in found for mask in masks(group)]
    return found


def masks(group):
    return [index << group[0] for index in range(1 << len(group))]


def swap(block, mask, count):
    return lax.ppermute(block, AXES, [(i, i ^ mask) for i in range(count)])


def gather_phase(own, group, count):
    return [own] + [swap(own, mask, count) for mask in masks(group)[1:]]


def split_rows(block, count):
    rows = block.shape[0] // count
    return [block[at * rows : (at + 1) * rows] for at in range(count)]


def added(sources, parts):
    return split_rows(sum(source.astype(F32) for source in sources).astype(BF), parts)


def combine_kernel(count, parts, loose, *refs):
    sources, outs = refs[:count], refs[count + loose : count + loose + parts]
    rows = outs[0].shape[0]
    for n, out in enumerate(outs):
        total = sources[0][n * rows : (n + 1) * rows].astype(F32)
        for source in sources[1:]:
            total = total + source[n * rows : (n + 1) * rows].astype(F32)
        out[...] = total.astype(BF)


def combine(sources, parts, after=(), through=()):
    rows, width = sources[0].shape
    rows //= parts
    if rows % BLOCK:
        return added(sources, parts) + list(through)
    return list(pl.pallas_call(
        functools.partial(combine_kernel, len(sources), parts, len(after) + len(through)),
        in_specs=[pl.BlockSpec(memory_space=pltpu.VMEM)] * len(sources) + [LOOSE] * (len(after) + len(through)),
        out_specs=[pl.BlockSpec(memory_space=pltpu.VMEM)] * parts + [LOOSE] * len(through),
        out_shape=[jax.ShapeDtypeStruct((rows, width), BF)] * parts + [jax.ShapeDtypeStruct(array.shape, array.dtype) for array in through],
        input_output_aliases={len(sources) + len(after) + n: parts + n for n in range(len(through))},
        compiler_params=pltpu.CompilerParams(vmem_limit_bytes=VMEM),
        cost_estimate=pl.CostEstimate(flops=10**6, bytes_accessed=sum(2 * source.size * 2 for source in sources), transcendentals=0),
        name="combine",
    )(*sources, *after, *through))


def exchange(parts, group, count):
    return [parts[0]] + [swap(part, mask, count) for part, mask in zip(parts[1:], masks(group)[1:])]


def scatter_core(pieces, count):
    pairs = list(zip(pieces[:PIECES], pieces[PIECES:]))
    sums = [None] * PIECES
    for n in (1, 2, 3, 0):
        keep, send = pairs[n]
        sums[n] = (keep.astype(F32) + swap(send, 1, count).astype(F32)).astype(BF)
    return sums


def local(
    inputs,
    segments,
    pad_mask,
    cotangent,
    w_query,
    b_query,
    w_key,
    w_value,
    b_value,
    w_out,
    b_out,
    gain_one,
    shift_one,
    w_up,
    b_up,
    w_down,
    b_down,
    gain_two,
    shift_two,
    pos_table,
):
    tokens = inputs.shape[0]
    narrow = lax.axis_size("narrow")
    wide = lax.axis_size("wide")
    count = wide * narrow
    me = lax.axis_index(AXES)
    groups = bit_groups(count)
    own_rows = D // count
    bits = count.bit_length() - 1
    places = [bits - 1 - bit for group in groups for bit in reversed(group)] + [bits, bits + 1]
    in_kernel = own_rows == BLOCK
    where = (me if in_kernel else jnp.zeros((), jnp.int32)).reshape(1).astype(jnp.int32)

    def flips(full):
        for axis in range(bits):
            mine = (me >> (bits - 1 - axis)) & 1
            full = jnp.where(mine == 1, jnp.flip(full, axis), full)
        return full

    def absolute(halves):
        if in_kernel:
            return halves
        full = jnp.concatenate(halves, axis=0).reshape([2] * bits + [own_rows, -1])
        full = flips(full.transpose([places.index(axis) for axis in range(bits + 2)])).reshape(D, -1)
        return full[: D // 2], full[D // 2 :]

    def relative(pieces):
        if in_kernel:
            return pieces
        full = flips(jnp.concatenate(pieces, axis=0).reshape([2] * bits + [own_rows, -1]))
        return split_rows(full.transpose(places).reshape(D, -1), 2 * PIECES)

    seg = segments.reshape(1, tokens)
    packs = tokens // PACK
    below = segments.reshape(packs, 1, PACK) < jnp.arange(ITEMS + 1, dtype=jnp.int32)[None, :, None]
    starts = jnp.sum(below.astype(jnp.int32), axis=2).reshape(packs * (ITEMS + 1))
    bias_width = b_up.shape[0]
    bias_piece = -(-bias_width // wide)
    own_a, own_b = pack(
        lax.axis_index("wide").astype(jnp.int32),
        bias_piece,
        (w_query.T, w_key.T, w_value.T, pos_table.T, w_out.T, w_up, w_down.T),
        b_up,
        (b_query, b_value, b_out, gain_one, shift_one, b_down, gain_two, shift_two),
    )
    gb = lax.all_gather(own_b, AXES, axis=0, tiled=True)
    for group in reversed(groups[1:]):
        own_a = jnp.concatenate(gather_phase(own_a, group, count), axis=0)
    a_halves = absolute(tuple(gather_phase(own_a, groups[0], count)))
    q, k, v, mixed, attn, picks, pt, vec, pieces = attend(where, starts, seg, inputs, a_halves, sines())
    bup = pieces.reshape(wide, narrow, own_rows, 128)[:, :, 0, 8 : 8 + bias_piece].transpose(1, 0, 2)
    bup = bup.reshape(narrow, wide * bias_piece)[:, :bias_width].reshape(1, FF)
    layer_out, d_first, d_attn, *grads_b = feed(narrow, own_rows, where, inputs, attn, cotangent, pad_mask, gb, vec, bup)
    parts_b = scatter_core(relative(grads_b), count)
    back = core_back(where, starts, q, k, v, d_attn, pt, inputs, mixed, picks, a_halves, parts_b)
    grads_a = relative(back[3:])
    next_parts = 1 << len(groups[2])
    parts_b = combine(exchange(parts_b, groups[1], count), next_parts, (), grads_a[PIECES:])
    grads_a = [*grads_a[:PIECES], *parts_b[next_parts:]]
    parts_b = parts_b[:next_parts]
    parts_a = scatter_core(grads_a, count)
    input_grad, held = input_grads(where, back[:3], d_first, a_halves, parts_a + parts_b[2:], parts_b[1])
    parts_b = [parts_b[0], held, *parts_b[2:]]
    parts_a = combine(exchange(parts_a, groups[1], count), 1 << len(groups[2]), [input_grad])
    for at in range(2, len(groups) - 1):
        next_parts = 1 << len(groups[at + 1])
        parts_b = added(exchange(parts_b, groups[at], count), next_parts)
        parts_a = added(exchange(parts_a, groups[at], count), next_parts)
    g_query, g_key, g_value, g_out, g_up, g_down, g_table, vectors, side = finish(
        exchange(parts_a, groups[-1], count), exchange(parts_b, groups[-1], count)
    )
    vectors = [vector.reshape(own_rows) for vector in vectors]
    grad_b_up = side[:, 8:].reshape(-1)[:bias_width]
    return (
        layer_out,
        input_grad,
        g_query.T,
        vectors[0],
        g_key.T,
        g_value.T,
        vectors[1],
        g_out.T,
        vectors[2],
        vectors[3],
        vectors[4],
        g_up,
        grad_b_up,
        g_down.T,
        vectors[5],
        vectors[6],
        vectors[7],
        g_table.T,
    )


def solution(mesh):
    both = P(("wide", "narrow"))
    rows = P(("wide", "narrow"), None)
    cols = P(None, ("wide", "narrow"))
    in_specs = (rows, both, both, rows, cols, both, cols, cols, both, cols, both, both, both, rows, P("narrow"), cols, both, both, both, cols)
    out_specs = (rows, rows, cols, both, cols, cols, both, cols, both, both, both, rows, P("narrow"), cols, both, both, both, cols)
    return jax.shard_map(local, mesh=mesh, in_specs=in_specs, out_specs=out_specs, check_vma=False)
```

```python
import functools
import math

import jax
import jax.numpy as jnp
import numpy as np
from jax import lax
from jax.experimental import pallas as pl
from jax.experimental.pallas import tpu as pltpu
from jax.sharding import PartitionSpec as P

D = 512
H = 8
FF = 3200
HD = 64
PACK = 640
LONG = 302
PLACES = 384
SCALE = 0.125
EPS = 1e-05
NEG = -1e9
WT = 3 * D + PLACES
WA = WT + 128
BLOCK = 16
BLOCKS = D // BLOCK
PIECES = 4
PIECE = D // (2 * PIECES)
WB = D + 2 * FF
TILE = 512
PARTS = 1
FF_CHUNKS = ((0, 1024), (1024, 1024), (2048, 1152))
ITEMS = 9
SHORT_WINDOW = (96, 128)
LONG_WINDOW = (320, 384)
SHORT_MOST = SHORT_WINDOW[0] - 15
PROB_ROWS = 992
GROUP = 4
GROUPS = H // GROUP
GD = GROUP * HD
PROB_COLS = GROUP * LONG_WINDOW[1]
AXES = ("wide", "narrow")
VMEM = 60 * 1024 * 1024
BF = jnp.bfloat16
F32 = jnp.float32


def nn(a, b):
    return lax.dot_general(a, b, (((1,), (0,)), ((), ())), preferred_element_type=F32)


def nt(a, b):
    return lax.dot_general(a, b, (((1,), (1,)), ((), ())), preferred_element_type=F32)


def item_masks(seg_row):
    wide = jnp.broadcast_to(seg_row.astype(F32), (8, PACK))
    col = jnp.transpose(wide)[:, 0:1]
    return col == wide[0:1]


def place_picks(same):
    lane = lax.broadcasted_iota(jnp.int32, (PACK, PACK), 1).astype(F32)
    first = jnp.min(jnp.where(same, lane, 1e6), axis=1, keepdims=True)
    place = lax.broadcasted_iota(jnp.int32, (PACK, 1), 0).astype(F32) - first
    slot = lax.broadcasted_iota(jnp.int32, (PACK, PLACES), 1).astype(F32)
    return jnp.where((place == slot) | (slot == PLACES - 1), 1.0, 0.0).astype(BF)


def each_item(starts_ref, pack, body):
    def visit(n, place):
        first = starts_ref[pack * (ITEMS + 1) + n]
        end = starts_ref[pack * (ITEMS + 1) + n + 1]
        length = end - first

        def window(sizes):
            spans = []
            for size in sizes:
                base = pl.multiple_of(jnp.minimum(lax.div(first, 16) * 16, PACK - size), 16)
                spans.append((size, pl.ds(base, size), first - base, end - base))
            body(*spans, pl.ds(pl.multiple_of(place, 16), sizes[0]))

        short = length <= SHORT_MOST

        @pl.when((length > 0) & short)
        def _():
            window(SHORT_WINDOW)

        @pl.when(length > SHORT_MOST)
        def _():
            window(LONG_WINDOW)

        return place + jnp.where(length > 0, jnp.where(short, SHORT_WINDOW[0], LONG_WINDOW[0]), 0)

    lax.fori_loop(0, ITEMS, visit, jnp.int32(0))


def by_head(block):
    lane = lax.broadcasted_iota(jnp.int32, block.shape, 1)
    zero = jnp.zeros_like(block)
    return jnp.concatenate([jnp.where((lane >= h * HD) & (lane < (h + 1) * HD), block, zero) for h in range(GROUP)], axis=0)


def heads_turned(left_t, right, size):
    parts = [nn(left_t[h * HD : (h + 1) * HD], right[:, h * size : (h + 1) * size]) for h in range(GROUP)]
    return jnp.concatenate(parts, axis=0)


GROUP_LANES = [slice(g * GD, (g + 1) * GD) for g in range(GROUPS)]


def block_rows(me_ref, place):
    owner = me_ref[0] ^ offsets(BLOCKS)[place]
    return pl.ds(pl.multiple_of(owner * BLOCK, BLOCK), BLOCK)


def block_loads(me_ref, halves, full_ref, sem):
    copies = []
    for place in range(BLOCKS):
        half, at = divmod(place, BLOCKS // 2)
        copies.append(pltpu.make_async_copy(halves[half].at[at * BLOCK : (at + 1) * BLOCK], full_ref.at[block_rows(me_ref, place)], sem))
    return copies


def load_blocks(me_ref, halves, full_ref, sem):
    copies = block_loads(me_ref, halves, full_ref, sem)
    for copy in copies:
        copy.start()
    for copy in copies:
        copy.wait()


def block_copies(me_ref, ref, col, width, pieces, sem):
    copies = []
    for place in range(BLOCKS):
        piece, at = divmod(place * BLOCK, PIECE)
        target = pieces[piece].at[at : at + BLOCK, col : col + width]
        copies.append(pltpu.make_async_copy(ref.at[block_rows(me_ref, place)], target, sem))
    return copies


def store_blocks(me_ref, ref, pieces, sem):
    copies = block_copies(me_ref, ref, 0, ref.shape[1], pieces, sem)
    for copy in copies:
        copy.start()
    for copy in copies:
        copy.wait()


def attend_kernel(me_ref, starts_ref, seg_ref, x_ref, al_ref, ar_ref, st_ref, q_ref, k_ref, v_ref, mix_ref, attn_ref, picks_ref, pt_ref, vec_ref, pieces_ref, ga_ref, hi_ref, lo_ref, sem):
    @pl.when(pl.program_id(0) == 0)
    def _():
        load_blocks(me_ref, (al_ref, ar_ref), ga_ref, sem)
        pieces_ref[...] = ga_ref[:, WT:].astype(F32)
        vec_ref[...] = jnp.transpose(pieces_ref[...])
        pos = st_ref[...] + ga_ref[:, 3 * D : 3 * D + PLACES].astype(F32)
        pos = jnp.where(lax.broadcasted_iota(jnp.int32, pos.shape, 1) < LONG, pos, 0.0)
        hi = pos.astype(BF)
        hi_ref[...] = hi
        lo_ref[...] = (pos - hi.astype(F32)).astype(BF)

    picks = place_picks(item_masks(seg_ref[...]))
    picks_ref[...] = picks
    x = x_ref[...]
    positions = nt(picks, hi_ref[...]) + nt(picks, lo_ref[...])
    mixed = (x.astype(F32) + positions).astype(BF)
    mix_ref[...] = mixed
    q_ref[...] = ((nt(mixed, ga_ref[:, 0:D]) + vec_ref[0:1]).astype(BF).astype(F32) * SCALE).astype(BF)
    k_ref[...] = nt(mixed, ga_ref[:, D : 2 * D]).astype(BF)
    v = (nt(x, ga_ref[:, 2 * D : 3 * D]) + vec_ref[1:2]).astype(BF)
    v_ref[...] = v
    attn_ref[...] = jnp.zeros_like(attn_ref)

    def item(key_span, query_span, store):
        keys, key_rows, low, high = key_span
        down = lax.broadcasted_iota(jnp.int32, (keys, 1), 0)
        shut = jnp.where((down >= low) & (down < high), 0.0, NEG)
        queries, query_rows, low, high = query_span
        across = lax.broadcasted_iota(jnp.int32, (1, queries), 1)
        live = jnp.where((across >= low) & (across < high), 1.0, 0.0)
        live = jnp.concatenate([live] * GROUP, axis=1)
        scores = [nt(k_ref[key_rows, lanes], by_head(q_ref[query_rows, lanes])) + shut for lanes in GROUP_LANES]
        probs = []
        for g in range(GROUPS):
            exps = jnp.exp(scores[g] - jnp.max(scores[g], axis=0, keepdims=True))
            scale = live / jnp.sum(exps, axis=0, keepdims=True)
            probs.append((exps * scale).astype(BF))
            pt_ref[0, g, store, 0 : GROUP * queries] = probs[g]
        for g, lanes in enumerate(GROUP_LANES):
            outs = heads_turned(jnp.transpose(v_ref[key_rows, lanes]), probs[g], queries)
            attn_ref[query_rows, lanes] += jnp.transpose(outs.astype(BF))

    each_item(starts_ref, pl.program_id(0), item)


def whole(shape):
    return pl.BlockSpec(shape, lambda i: tuple(0 for _ in shape), pipeline_mode=pl.Buffered(1))


def rows_of(count, width):
    return pl.BlockSpec((count, width), lambda i: (i, 0))


SCALAR = pl.BlockSpec(memory_space=pltpu.SMEM)
LOOSE = pl.BlockSpec(memory_space=pl.ANY)


def attend(where, starts, seg, x, halves, st):
    tokens = seg.shape[1]
    packs = tokens // PACK
    low = jax.ShapeDtypeStruct((tokens, D), BF)
    return pl.pallas_call(
        attend_kernel,
        grid=(packs,),
        in_specs=[SCALAR, SCALAR, pl.BlockSpec((1, PACK), lambda i: (0, i)), rows_of(PACK, D), LOOSE, LOOSE, whole((D, PLACES))],
        out_specs=[rows_of(PACK, D)] * 5 + [rows_of(PACK, PLACES), pl.BlockSpec((1, GROUPS, PROB_ROWS, PROB_COLS), lambda i: (i, 0, 0, 0)), whole((128, D)), whole((D, 128))],
        out_shape=[low] * 5
        + [
            jax.ShapeDtypeStruct((tokens, PLACES), BF),
            jax.ShapeDtypeStruct((packs, GROUPS, PROB_ROWS, PROB_COLS), BF), jax.ShapeDtypeStruct((128, D), F32), jax.ShapeDtypeStruct((D, 128), F32)],
        scratch_shapes=[
            pltpu.VMEM((D, WA), BF),
            pltpu.VMEM((D, PLACES), BF),
            pltpu.VMEM((D, PLACES), BF),
            pltpu.SemaphoreType.DMA,
        ],
        compiler_params=pltpu.CompilerParams(vmem_limit_bytes=VMEM),
        cost_estimate=pl.CostEstimate(flops=40 * 10**9, bytes_accessed=50 * 10**6, transcendentals=0),
        name="attend",
    )(where, starts, seg, x, *halves, st)


def centre(v):
    c = v - jnp.mean(v, axis=-1, keepdims=True)
    r = lax.rsqrt(jnp.mean(c * c, axis=-1, keepdims=True) + EPS)
    return c * r, r


def norm_back(g, n, r):
    return r * (g - jnp.mean(g, axis=-1, keepdims=True) - n * jnp.mean(g * n, axis=-1, keepdims=True))


def col_sum(v):
    return jnp.sum(v, axis=0, keepdims=True)


GELU_A = math.sqrt(2.0 / math.pi)
GELU_B = 0.044715


def feed_kernel(narrow, own_rows, me_ref, x_ref, attn_ref, cot_ref, pad_ref, gb_hbm, vec_ref, bup_ref, out_ref, dfirst_ref, dattn_ref, *refs):
    pieces, scratch = refs[: 2 * PIECES], refs[2 * PIECES :]
    gb_ref, act_ref, slope_ref, up_acc, down_acc, wo_acc, wo_low, side_ref, gv_ref, gbu_ref, sem, load_sems = scratch
    loads = [
        pltpu.make_async_copy(gb_hbm.at[:, at : at + size], gb_ref.at[:, at : at + size], load_sems.at[n])
        for n, (at, size) in enumerate(((0, D), (D, FF), (D + FF, FF)))
    ]
    step = pl.program_id(0)

    @pl.when(step == 0)
    def _():
        for copy in loads:
            copy.start()
        up_acc[...] = jnp.zeros_like(up_acc)
        down_acc[...] = jnp.zeros_like(down_acc)
        wo_acc[...] = jnp.zeros_like(wo_acc)
        gv_ref[...] = jnp.zeros_like(gv_ref)
        gbu_ref[...] = jnp.zeros_like(gbu_ref)
        loads[0].wait()

    gain_one, gain_two = vec_ref[3:4], vec_ref[6:7]
    keep_all = jnp.transpose(jnp.broadcast_to(pad_ref[...].astype(F32), (8, TILE)))[:, 0:1]
    parts = [slice(at, at + TILE // PARTS) for at in range(0, TILE, TILE // PARTS)]
    hidden, norm_one, r_one, hidden_t = {}, {}, {}, {}
    d_second, d_ff_t, d_hidden, d_branch_t, ff = {}, {}, {}, {}, {}

    def enter(p):
        rows = parts[p]
        first_sum = x_ref[rows].astype(F32) + (nt(attn_ref[rows], gb_ref[:, 0:D]) + vec_ref[2:3])
        norm_one[p], r_one[p] = centre(first_sum)
        hidden[p] = gain_one * norm_one[p] + vec_ref[4:5]

    def ahead(p):
        rows = parts[p]
        hidden_low = hidden[p].astype(BF)
        hidden_t[p] = jnp.transpose(hidden_low)
        ff[p] = 0.0
        for start, size in FF_CHUNKS:
            cols = slice(start, start + size)
            u = nn(hidden_low, gb_ref[:, D + start : D + start + size]) + bup_ref[0:1, cols]
            u2 = u * u
            t = jnp.tanh(u * (GELU_A + GELU_A * GELU_B * u2))
            h = 0.5 + 0.5 * t
            act = (u * h).astype(BF)
            act_ref[rows, cols] = act
            slope_ref[rows, cols] = (h + (u * h) * (1.0 - t) * (GELU_A + 3.0 * GELU_A * GELU_B * u2)).astype(BF)
            ff[p] = ff[p] + nt(act, gb_ref[:, D + FF + start : D + FF + start + size])

    def turn(p):
        rows = parts[p]
        keep = keep_all[rows]
        norm_two, r_two = centre(hidden[p] + (ff[p] + vec_ref[5:6]))
        out_ref[rows] = ((gain_two * norm_two + vec_ref[7:8]) * keep).astype(BF)
        top = cot_ref[rows].astype(F32) * keep
        gv_ref[6:7] += col_sum(top * norm_two)
        gv_ref[7:8] += col_sum(top)
        d_second[p] = norm_back(top * gain_two, norm_two, r_two)

    def behind(p):
        rows = parts[p]
        d_ff = d_second[p].astype(BF)
        gv_ref[5:6] += col_sum(d_ff.astype(F32))
        d_ff_t[p] = jnp.transpose(d_ff)
        d_hidden[p] = d_second[p]
        for start, size in FF_CHUNKS:
            cols = slice(start, start + size)
            d_act = nn(d_ff, gb_ref[:, D + FF + start : D + FF + start + size])
            d_pre = (slope_ref[rows, cols].astype(F32) * d_act).astype(BF)
            slope_ref[rows, cols] = d_pre
            gbu_ref[0:1, cols] += col_sum(d_pre.astype(F32))
            d_hidden[p] = d_hidden[p] + nt(d_pre, gb_ref[:, D + start : D + start + size])

    def leave(p):
        rows = parts[p]
        gv_ref[3:4] += col_sum(d_hidden[p] * norm_one[p])
        gv_ref[4:5] += col_sum(d_hidden[p])
        d_first = norm_back(d_hidden[p] * gain_one, norm_one[p], r_one[p])
        dfirst_ref[rows] = d_first
        d_branch = d_first.astype(BF)
        gv_ref[2:3] += col_sum(d_branch.astype(F32))
        d_branch_t[p] = jnp.transpose(d_branch)
        dattn_ref[rows] = nn(d_branch, gb_ref[:, 0:D]).astype(BF)

    def joined(pieces):
        return jnp.concatenate([pieces[p] for p in range(PARTS)], axis=1)

    def weights():
        ff_t, low_t = joined(d_ff_t), joined(hidden_t)
        for start, size in FF_CHUNKS:
            cols = slice(start, start + size)
            down_acc[:, cols] += nn(ff_t, act_ref[:, cols])
            up_acc[:, cols] += nn(low_t, slope_ref[:, cols])

    enter(0)

    @pl.when(step == 0)
    def _():
        loads[1].wait()
        loads[2].wait()

    ahead(0)
    turn(0)
    behind(0)
    leave(0)
    weights()
    wo_acc[...] += nn(joined(d_branch_t), attn_ref[...])

    @pl.when(step == pl.num_programs(0) - 1)
    def _():
        def send(ref, at, size):
            copies = block_copies(me_ref, ref, at, size, pieces, sem)
            for copy in copies:
                copy.start()
            return copies

        act_ref[...] = up_acc[...].astype(BF)
        copies = send(act_ref, D, FF)
        slope_ref[...] = down_acc[...].astype(BF)
        copies += send(slope_ref, D + FF, FF)
        wo_low[...] = wo_acc[...].astype(BF)
        copies += send(wo_low, 0, D)
        side = side_columns(narrow, own_rows, gbu_ref, side_ref.shape[1])
        vectors = jnp.transpose(jnp.concatenate([gv_ref[...], jnp.zeros((120, D), F32)], axis=0))
        first = side[:, 0:128] + vectors
        side_ref[:, 0:128] = first.astype(BF)
        if side_ref.shape[1] > 128:
            side_ref[:, 128:] = side[:, 128:].astype(BF)
        copies += send(side_ref, WB, side_ref.shape[1])
        for copy in copies:
            copy.wait()


def side_columns(narrow, own_rows, sums_ref, width):
    span = sums_ref.shape[1]
    bias = FF // narrow
    lane = lax.broadcasted_iota(jnp.int32, (1, width), 1)
    lines = []
    for n in range(narrow):
        for r in range(own_rows):
            at = r * (width - 8)
            if at < bias:
                moved = pltpu.roll(sums_ref[...], (span + 8 - n * bias - at) % span, 1)[0:1, 0:width]
                lines.append(jnp.where((lane >= 8) & (lane - 8 + at < bias), moved, 0.0))
            else:
                lines.append(jnp.zeros((1, width), F32))
    block = jnp.concatenate(lines, axis=0)
    return jnp.concatenate([block] * (D // block.shape[0]), axis=0)


def side_width(narrow, own_rows):
    return -(-(8 + -(-(FF // narrow) // own_rows)) // 128) * 128


def feed(narrow, own_rows, where, x, attn, cot, pad, gb, vec, bup):
    tokens = x.shape[0]
    side = side_width(narrow, own_rows)
    return pl.pallas_call(
        functools.partial(feed_kernel, narrow, own_rows),
        grid=(tokens // TILE,),
        in_specs=[
            SCALAR,
            rows_of(TILE, D),
            rows_of(TILE, D),
            rows_of(TILE, D),
            pl.BlockSpec((1, TILE), lambda i: (0, i)),
            LOOSE,
            whole((128, D)),
            whole((1, FF)),
        ],
        out_specs=[rows_of(TILE, D), rows_of(TILE, D), rows_of(TILE, D)] + [LOOSE] * (2 * PIECES),
        out_shape=[
            jax.ShapeDtypeStruct((tokens, D), BF),
            jax.ShapeDtypeStruct((tokens, D), F32),
            jax.ShapeDtypeStruct((tokens, D), BF),
        ]
        + [jax.ShapeDtypeStruct((PIECE, WB + side), BF)] * (2 * PIECES),
        scratch_shapes=[
            pltpu.VMEM((D, WB), BF),
            pltpu.VMEM((TILE, FF), BF),
            pltpu.VMEM((TILE, FF), BF),
            pltpu.VMEM((D, FF), F32),
            pltpu.VMEM((D, FF), F32),
            pltpu.VMEM((D, D), F32),
            pltpu.VMEM((D, D), BF),
            pltpu.VMEM((D, side), BF),
            pltpu.VMEM((8, D), F32),
            pltpu.VMEM((8, FF + 128), F32),
            pltpu.SemaphoreType.DMA,
            pltpu.SemaphoreType.DMA((3,)),
        ],
        compiler_params=pltpu.CompilerParams(vmem_limit_bytes=VMEM),
        cost_estimate=pl.CostEstimate(flops=80 * 10**9, bytes_accessed=40 * 10**6, transcendentals=0),
        name="feed",
    )(where, x, attn, cot, pad.reshape(1, tokens), gb, vec, bup)


def tn(a, b):
    return lax.dot_general(a, b, (((0,), (0,)), ((), ())), preferred_element_type=F32)


ACC = 3 * D + 2 * PLACES + 128


def core_kernel(me_ref, starts_ref, q_ref, k_ref, v_ref, dattn_ref, pt_ref, x_ref, mix_ref, picks_ref, al_ref, ar_ref, *refs):
    dq_ref, dk_ref, dv_ref, *pieces, acc, ga_ref, gw_ref, sem, load_sem = refs[-(3 + 2 * PIECES + 5) :]
    step = pl.program_id(0)

    loads = block_loads(me_ref, (al_ref, ar_ref), ga_ref, load_sem)

    @pl.when(step == 0)
    def _():
        for copy in loads:
            copy.start()
        acc[...] = jnp.zeros_like(acc)

    for ref in (dq_ref, dk_ref, dv_ref):
        ref[...] = jnp.zeros_like(ref)

    def item(key_span, query_span, store):
        key_rows = key_span[1]
        queries, query_rows = query_span[:2]
        d_outs = [by_head(dattn_ref[query_rows, lanes]) for lanes in GROUP_LANES]
        d_probs = [nt(v_ref[key_rows, lanes], d_outs[g]) for g, lanes in enumerate(GROUP_LANES)]
        probs = [pt_ref[0, g, store, 0 : GROUP * queries] for g in range(GROUPS)]
        d_scores = []
        for g in range(GROUPS):
            wide = probs[g].astype(F32)
            delta = jnp.sum(wide * d_probs[g], axis=0, keepdims=True)
            d_scores.append((wide * (d_probs[g] - delta)).astype(BF))
        for g, lanes in enumerate(GROUP_LANES):
            dv_ref[key_rows, lanes] += nn(probs[g], d_outs[g]).astype(BF)
            dk_ref[key_rows, lanes] += nn(d_scores[g], by_head(q_ref[query_rows, lanes])).astype(BF)
            d_queries = heads_turned(jnp.transpose(k_ref[key_rows, lanes]), d_scores[g], queries) * SCALE
            dq_ref[query_rows, lanes] += jnp.transpose(d_queries.astype(BF))

    each_item(starts_ref, step, item)
    dq_t, dk_t, dv_t = (jnp.transpose(ref[...]) for ref in (dq_ref, dk_ref, dv_ref))
    mixed, picks = mix_ref[...], picks_ref[...]
    acc[:, 0:D] += nn(dq_t, mixed)
    acc[:, D : 2 * D] += nn(dk_t, mixed)
    acc[:, 2 * D : 3 * D] += nn(dv_t, x_ref[...])
    acc[:, 3 * D : 3 * D + PLACES] += nn(dq_t, picks)
    acc[:, 3 * D + PLACES : 3 * D + 2 * PLACES] += nn(dk_t, picks)
    acc[:, 3 * D + 2 * PLACES :] += nn(dv_t, jnp.ones((PACK, 128), BF))

    @pl.when(step == pl.num_programs(0) - 1)
    def _():
        for copy in loads:
            copy.wait()
        gw_ref[:, 0 : 3 * D] = acc[:, 0 : 3 * D].astype(BF)
        table = tn(ga_ref[:, 0:D], acc[:, 3 * D : 3 * D + PLACES].astype(BF))
        table = table + tn(ga_ref[:, D : 2 * D], acc[:, 3 * D + PLACES : 3 * D + 2 * PLACES].astype(BF))
        gw_ref[:, 3 * D : WT] = table.astype(BF)
        lane = lax.broadcasted_iota(jnp.int32, (D, 128), 1)
        query_sum = acc[:, 3 * D + PLACES - 1 : 3 * D + PLACES]
        sums = jnp.where(lane == 0, query_sum, jnp.where(lane == 1, acc[:, 3 * D + 2 * PLACES :], 0.0))
        gw_ref[:, WT:] = sums.astype(BF)
        store_blocks(me_ref, gw_ref, pieces, sem)


def core_back(where, starts, q, k, v, d_attn, pt, x, mixed, picks, halves, after):
    tokens = x.shape[0]
    probs = pl.BlockSpec((1, GROUPS, PROB_ROWS, PROB_COLS), lambda i: (i, 0, 0, 0))
    flat = rows_of(PACK, D)
    return pl.pallas_call(
        core_kernel,
        grid=(tokens // PACK,),
        in_specs=[SCALAR, SCALAR] + [flat] * 4 + [probs, flat, flat, rows_of(PACK, PLACES)] + [LOOSE] * (2 + len(after)),
        out_specs=[flat] * 3 + [LOOSE] * (2 * PIECES),
        out_shape=[jax.ShapeDtypeStruct((tokens, D), BF)] * 3 + [jax.ShapeDtypeStruct((PIECE, WA), BF)] * (2 * PIECES),
        scratch_shapes=[
            pltpu.VMEM((D, ACC), F32),
            pltpu.VMEM((D, WA), BF),
            pltpu.VMEM((D, WA), BF),
            pltpu.SemaphoreType.DMA,
            pltpu.SemaphoreType.DMA,
        ],
        compiler_params=pltpu.CompilerParams(vmem_limit_bytes=VMEM),
        cost_estimate=pl.CostEstimate(flops=50 * 10**9, bytes_accessed=50 * 10**6, transcendentals=0),
        name="core_back",
    )(where, starts, q, k, v, d_attn, pt, x, mixed, picks, *halves, *after)


def inputs_kernel(me_ref, dq_ref, dk_ref, dv_ref, dfirst_ref, al_ref, ar_ref, *refs):
    out_ref, _, ga_ref, sem = refs[-4:]

    @pl.when(pl.program_id(0) == 0)
    def _():
        load_blocks(me_ref, (al_ref, ar_ref), ga_ref, sem)

    d_mixed = nn(dq_ref[...], ga_ref[:, 0:D]) + nn(dk_ref[...], ga_ref[:, D : 2 * D])
    out_ref[...] = (dfirst_ref[...] + d_mixed + nn(dv_ref[...], ga_ref[:, 2 * D : 3 * D])).astype(BF)


def input_grads(where, flat, d_first, halves, after, through):
    tokens = d_first.shape[0]
    return pl.pallas_call(
        inputs_kernel,
        grid=(tokens // PACK,),
        in_specs=[SCALAR] + [rows_of(PACK, D)] * 4 + [LOOSE] * (3 + len(after)),
        out_specs=[rows_of(PACK, D), LOOSE],
        out_shape=[jax.ShapeDtypeStruct((tokens, D), BF), jax.ShapeDtypeStruct(through.shape, through.dtype)],
        input_output_aliases={7 + len(after): 1},
        scratch_shapes=[pltpu.VMEM((D, WA), BF), pltpu.SemaphoreType.DMA],
        compiler_params=pltpu.CompilerParams(vmem_limit_bytes=VMEM),
        cost_estimate=pl.CostEstimate(flops=8 * 10**9, bytes_accessed=20 * 10**6, transcendentals=0),
        name="input_grads",
    )(where, *flat, d_first, *halves, *after, through)


def finish_kernel(count, *refs):
    a_refs, b_refs, outs, turn_ref = refs[:count], refs[count : 2 * count], refs[2 * count : -1], refs[-1]

    def total(pieces, start, size):
        result = pieces[0][:, start : start + size].astype(F32)
        for piece in pieces[1:]:
            result = result + piece[:, start : start + size].astype(F32)
        return result

    query, key, value, out, up, down, table = outs[:7]
    for at, ref in enumerate((query, key, value)):
        ref[...] = total(a_refs, at * D, D)
    out[...] = total(b_refs, 0, D)
    up[...] = total(b_refs, D, FF)
    down[...] = total(b_refs, D + FF, FF)
    table[...] = total(a_refs, 3 * D, PLACES)[:, 0:LONG]
    rows = query.shape[0]
    side = total(b_refs, WB, outs[-1].shape[1])
    outs[-1][...] = side
    lane = lax.broadcasted_iota(jnp.int32, (rows, 128), 1)
    turn_ref[...] = jnp.zeros_like(turn_ref)
    turn_ref[0:rows] = jnp.where(lane < 2, total(a_refs, WT, 128), side[:, 0:128])
    turned = jnp.transpose(turn_ref[...])
    for n, ref in enumerate(outs[7:15]):
        ref[...] = turned[n : n + 1, 0:rows]


def finish(a_parts, b_parts):
    rows = a_parts[0].shape[0]
    widths = [D, D, D, D, FF, FF, LONG]
    shapes = [(rows, width) for width in widths] + [(1, rows)] * 8 + [(rows, b_parts[0].shape[1] - WB)]
    vmem = pl.BlockSpec(memory_space=pltpu.VMEM)
    outs = pl.pallas_call(
        functools.partial(finish_kernel, len(a_parts)),
        in_specs=[vmem] * (2 * len(a_parts)),
        out_specs=[vmem] * len(shapes),
        out_shape=[jax.ShapeDtypeStruct(shape, F32) for shape in shapes],
        scratch_shapes=[pltpu.VMEM((128, 128), F32)],
        name="finish",
    )(*a_parts, *b_parts)
    return (*outs[:7], outs[7:15], outs[15])


def sines():
    half = D // 2
    frequency = np.exp(np.arange(half, dtype=np.float32) * np.float32(-2.0 * math.log(10000.0) / D))
    angles = frequency[:, None] * np.arange(PLACES, dtype=np.float32)[None, :]
    return jnp.asarray(np.concatenate([np.sin(angles), np.cos(angles)], axis=0).astype(np.float32))


def pack_kernel(piece, wide_ref, wq_ref, wk_ref, wv_ref, table_ref, wo_ref, up_ref, down_ref, bup_ref, *refs):
    vectors, (a_ref, b_ref, turn_ref, bias_ref) = refs[:8], refs[8:]
    rows = a_ref.shape[0]
    a_ref[:, 0:D] = wq_ref[...]
    a_ref[:, D : 2 * D] = wk_ref[...]
    a_ref[:, 2 * D : 3 * D] = wv_ref[...]
    a_ref[:, 3 * D : WT] = jnp.zeros((rows, PLACES), BF)
    a_ref[:, 3 * D : 3 * D + LONG] = table_ref[...]
    b_ref[:, 0:D] = wo_ref[...]
    b_ref[:, D : D + FF] = up_ref[...]
    b_ref[:, D + FF :] = down_ref[...]
    turn_ref[...] = jnp.zeros_like(turn_ref)
    for n, vector in enumerate(vectors):
        turn_ref[n : n + 1, 0:rows] = vector[...].astype(F32)
    bias_ref[...] = jnp.zeros_like(bias_ref)
    bias_ref[0:1, 0 : bup_ref.shape[1]] = bup_ref[...].astype(F32)
    span = bias_ref.shape[1]
    shift = lax.rem(span + 8 - wide_ref[0] * piece, span)
    moved = pltpu.roll(bias_ref[...], shift, 1)[0:1, 0:128]
    lane = lax.broadcasted_iota(jnp.int32, (rows, 128), 1)
    row = lax.broadcasted_iota(jnp.int32, (rows, 128), 0)
    mine = (row == 0) & (lane >= 8) & (lane < 8 + piece)
    columns = jnp.transpose(turn_ref[...])[0:rows]
    a_ref[:, WT:] = jnp.where(mine, moved, columns).astype(BF)


def pack(wide_index, piece, matrices, b_up, vectors):
    rows = matrices[0].shape[0]
    span = -(-(b_up.shape[0] + 8) // 128) * 128
    return pl.pallas_call(
        functools.partial(pack_kernel, piece),
        in_specs=[SCALAR] + [pl.BlockSpec(memory_space=pltpu.VMEM)] * 16,
        out_specs=[pl.BlockSpec(memory_space=pltpu.VMEM)] * 2,
        out_shape=[jax.ShapeDtypeStruct((rows, WA), BF), jax.ShapeDtypeStruct((rows, WB), BF)],
        scratch_shapes=[pltpu.VMEM((128, 128), F32), pltpu.VMEM((8, span), F32)],
        name="pack",
    )(wide_index.reshape(1), *matrices, b_up.reshape(1, -1), *[vector.reshape(1, rows) for vector in vectors])


def bit_groups(count):
    bits = count.bit_length() - 1
    return [(0,)] + [tuple(range(at, min(at + 2, bits))) for at in range(1, bits, 2)]


def offsets(count):
    found = [0]
    for group in bit_groups(count):
        found = [old | mask for old in found for mask in masks(group)]
    return found


def masks(group):
    return [index << group[0] for index in range(1 << len(group))]


def swap(block, mask, count):
    return lax.ppermute(block, AXES, [(i, i ^ mask) for i in range(count)])


def gather_phase(own, group, count):
    return [own] + [swap(own, mask, count) for mask in masks(group)[1:]]


def split_rows(block, count):
    rows = block.shape[0] // count
    return [block[at * rows : (at + 1) * rows] for at in range(count)]


def added(sources, parts):
    return split_rows(sum(source.astype(F32) for source in sources).astype(BF), parts)


def combine_kernel(count, parts, loose, *refs):
    sources, outs = refs[:count], refs[count + loose : count + loose + parts]
    rows = outs[0].shape[0]
    for n, out in enumerate(outs):
        total = sources[0][n * rows : (n + 1) * rows].astype(F32)
        for source in sources[1:]:
            total = total + source[n * rows : (n + 1) * rows].astype(F32)
        out[...] = total.astype(BF)


def combine(sources, parts, after=(), through=()):
    rows, width = sources[0].shape
    rows //= parts
    if rows % BLOCK:
        return added(sources, parts) + list(through)
    return list(pl.pallas_call(
        functools.partial(combine_kernel, len(sources), parts, len(after) + len(through)),
        in_specs=[pl.BlockSpec(memory_space=pltpu.VMEM)] * len(sources) + [LOOSE] * (len(after) + len(through)),
        out_specs=[pl.BlockSpec(memory_space=pltpu.VMEM)] * parts + [LOOSE] * len(through),
        out_shape=[jax.ShapeDtypeStruct((rows, width), BF)] * parts + [jax.ShapeDtypeStruct(array.shape, array.dtype) for array in through],
        input_output_aliases={len(sources) + len(after) + n: parts + n for n in range(len(through))},
        compiler_params=pltpu.CompilerParams(vmem_limit_bytes=VMEM),
        cost_estimate=pl.CostEstimate(flops=10**6, bytes_accessed=sum(2 * source.size * 2 for source in sources), transcendentals=0),
        name="combine",
    )(*sources, *after, *through))


def exchange(parts, group, count):
    return [parts[0]] + [swap(part, mask, count) for part, mask in zip(parts[1:], masks(group)[1:])]


def scatter_core(pieces, count):
    pairs = list(zip(pieces[:PIECES], pieces[PIECES:]))
    sums = [None] * PIECES
    for n in (1, 2, 3, 0):
        keep, send = pairs[n]
        sums[n] = (keep.astype(F32) + swap(send, 1, count).astype(F32)).astype(BF)
    return sums


def local(
    inputs,
    segments,
    pad_mask,
    cotangent,
    w_query,
    b_query,
    w_key,
    w_value,
    b_value,
    w_out,
    b_out,
    gain_one,
    shift_one,
    w_up,
    b_up,
    w_down,
    b_down,
    gain_two,
    shift_two,
    pos_table,
):
    tokens = inputs.shape[0]
    narrow = lax.axis_size("narrow")
    wide = lax.axis_size("wide")
    count = wide * narrow
    me = lax.axis_index(AXES)
    groups = bit_groups(count)
    own_rows = D // count
    bits = count.bit_length() - 1
    places = [bits - 1 - bit for group in groups for bit in reversed(group)] + [bits, bits + 1]
    in_kernel = own_rows == BLOCK
    where = (me if in_kernel else jnp.zeros((), jnp.int32)).reshape(1).astype(jnp.int32)

    def flips(full):
        for axis in range(bits):
            mine = (me >> (bits - 1 - axis)) & 1
            full = jnp.where(mine == 1, jnp.flip(full, axis), full)
        return full

    def absolute(halves):
        if in_kernel:
            return halves
        full = jnp.concatenate(halves, axis=0).reshape([2] * bits + [own_rows, -1])
        full = flips(full.transpose([places.index(axis) for axis in range(bits + 2)])).reshape(D, -1)
        return full[: D // 2], full[D // 2 :]

    def relative(pieces):
        if in_kernel:
            return pieces
        full = flips(jnp.concatenate(pieces, axis=0).reshape([2] * bits + [own_rows, -1]))
        return split_rows(full.transpose(places).reshape(D, -1), 2 * PIECES)

    seg = segments.reshape(1, tokens)
    packs = tokens // PACK
    below = segments.reshape(packs, 1, PACK) < jnp.arange(ITEMS + 1, dtype=jnp.int32)[None, :, None]
    starts = jnp.sum(below.astype(jnp.int32), axis=2).reshape(packs * (ITEMS + 1))
    bias_width = b_up.shape[0]
    bias_piece = -(-bias_width // wide)
    own_a, own_b = pack(
        lax.axis_index("wide").astype(jnp.int32),
        bias_piece,
        (w_query.T, w_key.T, w_value.T, pos_table.T, w_out.T, w_up, w_down.T),
        b_up,
        (b_query, b_value, b_out, gain_one, shift_one, b_down, gain_two, shift_two),
    )
    gb = lax.all_gather(own_b, AXES, axis=0, tiled=True)
    for group in reversed(groups[1:]):
        own_a = jnp.concatenate(gather_phase(own_a, group, count), axis=0)
    a_halves = absolute(tuple(gather_phase(own_a, groups[0], count)))
    q, k, v, mixed, attn, picks, pt, vec, pieces = attend(where, starts, seg, inputs, a_halves, sines())
    bup = pieces.reshape(wide, narrow, own_rows, 128)[:, :, 0, 8 : 8 + bias_piece].transpose(1, 0, 2)
    bup = bup.reshape(narrow, wide * bias_piece)[:, :bias_width].reshape(1, FF)
    layer_out, d_first, d_attn, *grads_b = feed(narrow, own_rows, where, inputs, attn, cotangent, pad_mask, gb, vec, bup)
    parts_b = scatter_core(relative(grads_b), count)
    back = core_back(where, starts, q, k, v, d_attn, pt, inputs, mixed, picks, a_halves, parts_b)
    grads_a = relative(back[3:])
    next_parts = 1 << len(groups[2])
    parts_b = combine(exchange(parts_b, groups[1], count), next_parts, (), grads_a[PIECES:])
    grads_a = [*grads_a[:PIECES], *parts_b[next_parts:]]
    parts_b = parts_b[:next_parts]
    parts_a = scatter_core(grads_a, count)
    input_grad, held = input_grads(where, back[:3], d_first, a_halves, parts_a + parts_b[2:], parts_b[1])
    parts_b = [parts_b[0], held, *parts_b[2:]]
    parts_a = combine(exchange(parts_a, groups[1], count), 1 << len(groups[2]), [input_grad])
    for at in range(2, len(groups) - 1):
        next_parts = 1 << len(groups[at + 1])
        parts_b = added(exchange(parts_b, groups[at], count), next_parts)
        parts_a = added(exchange(parts_a, groups[at], count), next_parts)
    g_query, g_key, g_value, g_out, g_up, g_down, g_table, vectors, side = finish(
        exchange(parts_a, groups[-1], count), exchange(parts_b, groups[-1], count)
    )
    vectors = [vector.reshape(own_rows) for vector in vectors]
    grad_b_up = side[:, 8:].reshape(-1)[:bias_width]
    return (
        layer_out,
        input_grad,
        g_query.T,
        vectors[0],
        g_key.T,
        g_value.T,
        vectors[1],
        g_out.T,
        vectors[2],
        vectors[3],
        vectors[4],
        g_up,
        grad_b_up,
        g_down.T,
        vectors[5],
        vectors[6],
        vectors[7],
        g_table.T,
    )


def solution(mesh):
    both = P(("wide", "narrow"))
    rows = P(("wide", "narrow"), None)
    cols = P(None, ("wide", "narrow"))
    in_specs = (rows, both, both, rows, cols, both, cols, cols, both, cols, both, both, both, rows, P("narrow"), cols, both, both, both, cols)
    out_specs = (rows, rows, cols, both, cols, cols, both, cols, both, both, both, rows, P("narrow"), cols, both, both, both, cols)
    return jax.shard_map(local, mesh=mesh, in_specs=in_specs, out_specs=out_specs, check_vma=False)
```
